256 devices in a mesh: exp: 32 (over z, y), head: 8 (over x, core).
Axes of the slice: x: 4, y: 4, z: 8, core: 2. Of those that a mesh axis runs over, the one named last changes fastest.
Arguments:
- tokens: bfloat16 [4096, 4096], P('exp', 'head'), may hold values from -6 to 6
- cotangent: bfloat16 [4096, 4096], P('exp', 'head'), may hold values from -3 to 3
- gates: bfloat16 [4096, 2], P('exp'), may hold values from 0.099609375 to 1
- expert_ids: int32 [4096, 2], P('exp'), may hold values from 0 to 31, all different within a row; in each aligned block of 128 rows (0 to 127, 128 to 255, ...) at most 16 rows name the same one
- w_up: bfloat16 [32, 4096, 2048], P('exp', None, 'head'), may hold values from -0.09375 to 0.09375
- w_down: bfloat16 [32, 2048, 4096], P('exp', 'head'), may hold values from -0.125 to 0.125
Outputs:
- grad_tokens: bfloat16 [4096, 4096], P('exp', 'head')
- grad_gates: bfloat16 [4096, 2], P('exp')
- grad_up: bfloat16 [32, 4096, 2048], P('exp', None, 'head')
- grad_down: bfloat16 [32, 2048, 4096], P('exp', 'head')
The draws below stay inside these ranges and needn't reach their ends.
Inputs may be any that keep to these rules, and one draw needn't show every extreme that they name: `expert_ids`: the two experts of a token differ; among the tokens of one index of exp, no expert is named more than 16 times, and in every draw some expert is named exactly 16 times by the tokens of some index.
All inputs are finite; a program needn't handle non-finite values.
Results may differ from the reference program's by a relative error of at most 0.0058.
Values may be sent and summed in bfloat16 or wider, within the bound.
A program may use at most 128 MiB of HBM per device.

```python
import math
import jax
import jax.numpy as jnp
import numpy as np
from jax import lax

D = 4096
FF = 2048
TOK_DEV = 128
EXPERTS = 32
TOKENS = 4096
CAP = 16
ROWS = 512
N_EXP = 32


def block_scale(rng, extent, cuts, least, largest):
    gain, own = 1.0, jax.random.fold_in(rng, 6)
    for dim, shards_of in cuts:
        heights = jnp.exp(jax.random.uniform(jax.random.fold_in(own, dim), (shards_of,), jnp.float32, least / len(cuts), largest / len(cuts)))
        gain = gain * jnp.repeat(heights, extent[dim] // shards_of).reshape([-1 if axis == dim else 1 for axis in range(len(extent))])
    return gain


def deal_out(key, own, number, rows, number_of, top, bound, skew):
    ranking = jax.random.permutation(key, number_of)
    heavy_load, ordinary = shares(number_of, rows * top, bound, skew, True), shares(number_of, rows * top, bound, skew, False)
    places = jnp.arange(number_of)

    def named(tallies, offset_by):
        used = int((tallies > 0).sum())
        fixed = max(1, used // 4)
        passed = fixed + (places - fixed + offset_by * (used - fixed)) % max(1, number_of - fixed)
        return jnp.zeros((number_of,), jnp.int32).at[ranking[jnp.where(places < fixed, places, passed)]].set(jnp.asarray(tallies, jnp.int32))

    tallies = jnp.where(number % 4 == 0, named(heavy_load, number // 4), named(ordinary, number - number // 4 - 1))
    mixed = jax.random.permutation(jax.random.fold_in(own, 3), number_of)
    giver, taker = mixed[0:number_of // 2 * 2:2], mixed[1:number_of // 2 * 2:2]
    margin = jnp.minimum(tallies[giver] - 1, bound - tallies[taker]) // 2
    margin = jnp.where((giver == ranking[0]) | (taker == ranking[0]) | (tallies[taker] == 0), 0, jnp.maximum(margin, 0))
    passed = jax.random.randint(jax.random.fold_in(own, 4), (number_of // 2,), 0, 1 << 20) % (margin + 1)
    tallies = tallies.at[giver].add(-passed).at[taker].add(passed)
    items = jnp.searchsorted(jnp.cumsum(tallies), jnp.arange(rows * top), side="right").astype(jnp.int32)
    listing = items.reshape(top, rows).T
    listing = listing[jax.random.permutation(jax.random.fold_in(own, 1), rows)]
    offset_by = jax.random.randint(jax.random.fold_in(own, 2), (rows, 1), 0, top)
    return jnp.take_along_axis(listing, (jnp.arange(top)[None, :] + offset_by) % top, axis=1)


def shares(number_of, total, bound, lean, full):
    weights = [(1 << 20) // math.isqrt(standing ** lean) + 1 for standing in range(1, number_of + 1)]
    largest = bound if full else min(bound, max(-(-total // number_of), total * weights[0] // sum(weights)))
    least = 1 if total - largest >= number_of - 1 else 0
    holding, spare = [largest] + [least] * (number_of - 1), total - largest - least * (number_of - 1)
    while spare > 0:
        free = [i for i in range(1, number_of) if holding[i] < largest] or [i for i in range(1, number_of) if holding[i] < bound]
        mass, remaining = sum([weights[i] for i in free]), spare
        for i in free:
            addition = min(bound - holding[i], max(1, remaining * weights[i] // mass), spare)
            holding[i] = holding[i] + addition
            spare = spare - addition
    return np.array(holding)


def gaussian(own_key, extent, deviation, reach, shards=(), kind=jnp.bfloat16):
    gain = block_scale(own_key, extent, shards, -0.22, 0.18) if shards else 1.0
    drawn = jax.random.normal(own_key, extent, jnp.float32) * deviation * gain
    return jnp.minimum(jnp.maximum(drawn, -reach), reach).astype(kind)


def setup_inputs(seed: int = 0) -> dict:
    keys = jax.random.split(jax.random.key(seed), 7)
    tokens = gaussian(keys[0], (TOKENS, D), 1.0, 6.0, ((0, 32), (1, 8)))
    cotangent = gaussian(keys[1], (TOKENS, D), 0.5, 3.0, ((0, 32), (1, 8)))
    gates = jnp.clip(0.099609375 + 0.9003906 * jax.random.uniform(keys[2], (TOKENS, 2), jnp.float32) ** block_scale(keys[2], (TOKENS, 2), ((0, 32),), -0.2, 0.2), 0.099609375, 1.0).astype(jnp.bfloat16)
    expert_ids_keys = jax.random.split(jax.random.fold_in(keys[3], 1), TOKENS // TOK_DEV)
    expert_ids_turns = jax.random.permutation(jax.random.fold_in(keys[3], 3), TOKENS // TOK_DEV)
    expert_ids = jax.vmap(lambda own, number: deal_out(jax.random.fold_in(keys[3], 2), own, number, TOK_DEV, EXPERTS, 2, CAP, 2))(expert_ids_keys, expert_ids_turns).reshape((TOKENS, 2))
    w_up = gaussian(keys[4], (EXPERTS, D, FF), D ** -0.5, 0.09375, ((0, 32), (2, 8)))
    w_down = gaussian(keys[5], (EXPERTS, FF, D), FF ** -0.5, 0.125, ((0, 32), (1, 8)))
    return {"tokens": tokens, "cotangent": cotangent, "gates": gates, "expert_ids": expert_ids, "w_up": w_up, "w_down": w_down}


def gelu_parts(pre):
    phi = 0.5 * (1.0 + lax.erf(pre / math.sqrt(2.0)))
    act = pre * phi
    slope = phi + pre * jnp.exp(-0.5 * pre * pre) / math.sqrt(2.0 * math.pi)
    return (act, slope)

def reference(tokens, cotangent, gates, expert_ids, w_up, w_down):
    count = 2 * TOKENS
    flat = expert_ids.reshape(N_EXP, 2 * TOK_DEV)
    onehot = (flat[:, :, None] == jnp.arange(EXPERTS, dtype=jnp.int32)[None, None, :]).astype(jnp.int32)
    before = jnp.cumsum(onehot, axis=1) - onehot
    slot = lax.optimization_barrier(jnp.sum(before * onehot, axis=2))
    source = jnp.arange(N_EXP, dtype=jnp.int32)[:, None]
    dest = (flat * (N_EXP * CAP) + source * CAP + slot).reshape(count).astype(jnp.int32)
    table = jnp.full((EXPERTS * ROWS,), count, jnp.int32).at[dest].set(jnp.arange(count, dtype=jnp.int32))
    x_pad = jnp.concatenate([tokens, jnp.zeros((1, D), tokens.dtype)], axis=0)
    dy_pad = jnp.concatenate([cotangent, jnp.zeros((1, D), cotangent.dtype)], axis=0)
    g_pad = jnp.concatenate([gates.reshape(count), jnp.zeros((1,), gates.dtype)], axis=0)

    def one_expert(items):
        index, weight_up, weight_down = items
        x_rows = x_pad[index // 2]
        dy_rows = dy_pad[index // 2]
        g_rows = g_pad[index].astype(jnp.float32)[:, None]
        pre = jnp.dot(x_rows, weight_up, preferred_element_type=jnp.float32)
        back = jnp.dot(dy_rows, weight_down.T, preferred_element_type=jnp.float32)
        act, slope = gelu_parts(pre)
        score = lax.optimization_barrier(jnp.sum(back * act, axis=1)).astype(jnp.bfloat16)
        scaled = (g_rows * act).astype(jnp.bfloat16)
        delta = (g_rows * back * slope).astype(jnp.bfloat16)
        grad_down = jnp.dot(scaled.T, dy_rows, preferred_element_type=jnp.float32).astype(jnp.bfloat16)
        grad_up = jnp.dot(x_rows.T, delta, preferred_element_type=jnp.float32).astype(jnp.bfloat16)
        row_grad = jnp.dot(delta, weight_up.T, preferred_element_type=jnp.float32).astype(jnp.bfloat16)
        return (row_grad, score, grad_up, grad_down)
    row_grad, score, grad_up, grad_down = lax.map(one_expert, (table.reshape(EXPERTS, ROWS), w_up, w_down))
    picked = row_grad.reshape(EXPERTS * ROWS, D)[dest].reshape(TOKENS, 2, D).astype(jnp.float32)
    grad_tokens = lax.optimization_barrier(jnp.sum(picked, axis=1)).astype(jnp.bfloat16)
    grad_gates = score.reshape(EXPERTS * ROWS)[dest].reshape(TOKENS, 2)
    return (grad_tokens, grad_gates, grad_up, grad_down)
```

```python
import math

import jax
import jax.numpy as jnp
from jax import lax
from jax.experimental import pallas as pl
from jax.experimental.pallas import tpu as pltpu
from jax.sharding import PartitionSpec as P

MESH = pl.DeviceIdType.MESH
BF16, F32, I32 = jnp.bfloat16, jnp.float32, jnp.int32

NZ, NY, NX = 8, 4, 4
EXP, HEAD = NZ * NY, 2 * NX
CAP = 16
TOK = 128
CH = NZ * CAP
NCH = NY
ROWS = NCH * CH
FL = 512
HID = 256
D = HEAD * FL
XD = 2 * FL
MSG = XD + 128
RET = FL + 128


def gelu_parts(pre):
    phi = 0.5 * (1.0 + lax.erf(pre * math.sqrt(0.5)))
    act = pre * phi
    slope = phi + pre * jnp.exp(-0.5 * pre * pre) * (1.0 / math.sqrt(2.0 * math.pi))
    return act, slope


def nn(a, b):
    return jnp.dot(a, b, preferred_element_type=F32)


def nt(a, b):
    return lax.dot_general(a, b, (((1,), (1,)), ((), ())), preferred_element_type=F32)


def tn(a, b):
    return lax.dot_general(a, b, (((0,), (0,)), ((), ())), preferred_element_type=F32)


def kernel(
    tok_ref, cot_ref, gates_ref, ids_ref, wup_hbm, wdn_hbm,
    gt_out, gg_out, gup_out, gdn_out,
    wup, wdn, gup, gdn, pt0, pt1, send, rows, scaled, delta,
    sib_send, sib_recv, own, m1s, m1r, m2s, m2r, sc_send, sc_recv, ret_send, ret_recv,
    w_sem, o_sem,
    d_send, d_recv, ga_send, ga_recv, gb_send, gb_recv, a2_send, a2_recv, b2_send, b2_recv,
    gs_send, gs_recv, sib_ss, sib_rs, m1_ss, m1_rs, m2_ss, m2_rs, sc_ss, sc_rs, r_ss, r_rs,
):
    e, h = lax.axis_index("exp"), lax.axis_index("head")
    z, y = e // NY, lax.rem(e, NY)
    x, c = h // 2, lax.rem(h, 2)

    def head_of(xx, cc):
        return lax.rem(xx + NX, NX) * 2 + cc

    right, left, opp = head_of(x + 1, c), head_of(x - 1, c), head_of(x + 2, c)
    sib = x * 2 + (1 - c)

    def exp_of(zz, yy):
        return lax.rem(zz + NZ, NZ) * NY + lax.rem(yy + NY, NY)

    barrier = pltpu.get_barrier_semaphore()

    def greet_exp(i, carry):
        pl.semaphore_signal(barrier, inc=1, device_id=(lax.rem(e + i, EXP), h), device_id_type=MESH)
        return carry

    def greet_head(i, carry):
        pl.semaphore_signal(barrier, inc=1, device_id=(e, lax.rem(h + i, HEAD)), device_id_type=MESH)
        return carry

    lax.fori_loop(1, EXP, greet_exp, 0)
    lax.fori_loop(1, HEAD, greet_head, 0)

    load_up = pltpu.make_async_copy(wup_hbm.at[0], wup, w_sem.at[0])
    load_dn = pltpu.make_async_copy(wdn_hbm.at[0], wdn, w_sem.at[1])
    load_up.start()
    load_dn.start()

    ids = ids_ref[...]

    def offset_of(expert):
        return ((y - (expert & (NY - 1))) & (NY - 1)) * NZ + ((z - (expert >> 2)) & (NZ - 1))

    r0, r1 = offset_of(ids[:, 0:1]), offset_of(ids[:, 1:2])
    lane = lax.broadcasted_iota(I32, (TOK, 128), 1)
    sub = lax.broadcasted_iota(I32, (TOK, 128), 0)
    oh0, oh1 = (r0 == lane).astype(F32), (r1 == lane).astype(F32)
    before = nn((lane < sub).astype(BF16), (oh0 + oh1).astype(BF16))
    d0 = r0 * CAP + jnp.sum(oh0 * before, axis=1, keepdims=True).astype(I32)
    d1 = r1 * CAP + jnp.sum(oh1 * before, axis=1, keepdims=True).astype(I32)
    slots = lax.broadcasted_iota(I32, (TOK, ROWS), 1)
    pt0[...] = (d0 == slots).astype(BF16)
    pt1[...] = (d1 == slots).astype(BF16)
    gates = gates_ref[...].astype(F32)
    gate0 = jnp.broadcast_to(gates[:, 0:1], (TOK, 128)).astype(BF16)
    gate1 = jnp.broadcast_to(gates[:, 1:2], (TOK, 128)).astype(BF16)

    def rows_of(k):
        return pl.ds(k * CH, CH)

    def block(p):
        return pl.ds(pl.multiple_of(p * CAP, CAP), CAP)

    def fill(k):
        here = rows_of(k)
        p0, p1 = pt0[:, here], pt1[:, here]
        both = p0 + p1
        send[here, 0:FL] = tn(both, tok_ref[...]).astype(BF16)
        send[here, FL:XD] = tn(both, cot_ref[...]).astype(BF16)
        send[here, XD:MSG] = (tn(p0, gate0) + tn(p1, gate1)).astype(BF16)

    def remote(src, dst, ss, rs, exp_i, head_i):
        return pltpu.make_async_remote_copy(
            src_ref=src, dst_ref=dst, send_sem=ss, recv_sem=rs,
            device_id=(exp_i, head_i), device_id_type=MESH,
        )

    def dispatch(k):
        def one(j, carry):
            p = k * NZ + j
            remote(
                send.at[block(p)], rows.at[h, block(p)], d_send.at[0], d_recv.at[k],
                exp_of(z - j, y - k), h,
            ).start()
            return carry

        lax.fori_loop(1 if k == 0 else 0, NZ, one, 0)

    def wait_recv(ref, rs):
        remote(ref, ref, rs, rs, e, sib).wait_recv()

    def wait_send(ref, ss):
        remote(ref, ref, ss, ss, e, sib).wait_send()

    fill(0)
    pl.semaphore_wait(barrier, EXP - 1 + HEAD - 1)
    dispatch(0)
    rows[h, 0:CAP, :] = send[0:CAP, :]
    for k in range(1, NCH):
        fill(k)
        dispatch(k)

    def part(hh, k, start=0, size=CH):
        return rows.at[hh, pl.ds(k * CH + start, size), pl.ds(0, XD)]

    half = CH // 2

    def gather1(k):
        if k == 0:
            wait_recv(rows.at[h, pl.ds(CAP, CH - CAP)], d_recv.at[k])
        else:
            wait_recv(rows.at[h, rows_of(k)], d_recv.at[k])
        mine = part(h, k)
        remote(mine, mine, ga_send.at[0], ga_recv.at[k], e, right).start()
        remote(mine, mine, gb_send.at[0], gb_recv.at[k], e, left).start()
        remote(mine, mine, gs_send.at[0], gs_recv.at[k, 0], e, sib).start()

    def gather2(k):
        low, high = part(left, k, 0, half), part(right, k, half, half)
        wait_recv(part(left, k), ga_recv.at[k])
        remote(low, low, a2_send.at[0], a2_recv.at[k], e, right).start()
        remote(part(left, k), part(left, k), gs_send.at[1], gs_recv.at[k, 1], e, sib).start()
        wait_recv(part(right, k), gb_recv.at[k])
        remote(high, high, b2_send.at[0], b2_recv.at[k], e, left).start()
        remote(part(right, k), part(right, k), gs_send.at[2], gs_recv.at[k, 2], e, sib).start()

    def gather3(k):
        wait_recv(part(opp, k, 0, half), a2_recv.at[k])
        wait_recv(part(opp, k, half, half), b2_recv.at[k])
        remote(part(opp, k), part(opp, k), gs_send.at[3], gs_recv.at[k, 3], e, sib).start()

    def gather4(k):
        for i in range(4):
            wait_recv(part(h, k), gs_recv.at[k, i])

    eye = lax.broadcasted_iota(I32, (CH, CH), 0) == lax.broadcasted_iota(I32, (CH, CH), 1)

    def features(hh):
        return pl.ds(pl.multiple_of(hh * FL, FL), FL)

    def compute(k):
        here = rows_of(k)

        def step(hh, sums):
            pre, back = sums
            pre = pre + nn(rows[hh, here, 0:FL], wup[features(hh), :])
            back = back + nt(rows[hh, here, FL:XD], wdn[:, features(hh)])
            return pre, back

        zero = jnp.zeros((CH, HID), F32)
        pre, back = lax.fori_loop(0, HEAD, step, (zero, zero))
        g = rows[h, here, XD:MSG][:, 0:1].astype(F32)
        act, slope = gelu_parts(pre)
        score = jnp.sum(back * act, axis=1, keepdims=True)
        scaled[here, :] = (g * act).astype(BF16)
        delta[here, :] = (g * back * slope).astype(BF16)

        def give(xx, carry):
            sib_send[k, xx] = nt(delta[here, :], wup[features(xx * 2 + (1 - c)), :]).astype(BF16)
            return carry

        lax.fori_loop(0, NX, give, 0)
        remote(sib_send.at[k], sib_recv.at[k], sib_ss.at[k], sib_rs.at[k], e, sib).start()
        line = jnp.sum(jnp.where(eye, score, 0.0), axis=0, keepdims=True)
        sc_send[k] = line
        sc_recv[k, h] = line

        def tell(i, carry):
            remote(
                sc_send.at[k], sc_recv.at[k, h], sc_ss.at[k], sc_rs.at[k], e, lax.rem(h + i, HEAD)
            ).start()
            return carry

        lax.fori_loop(1, HEAD, tell, 0)

        def keep(xx, carry):
            own[k, xx] = nt(delta[here, :], wup[features(xx * 2 + c), :])
            return carry

        lax.fori_loop(0, NX, keep, 0)

    def pair(k, xx, start, size):
        at = lax.rem(xx + NX, NX)
        cols = pl.ds(start, size)
        return own[k, at, :, cols] + sib_recv[k, at, :, cols].astype(F32)

    hf = FL // 2

    def reduce1(k):
        wait_recv(sib_recv.at[k], sib_rs.at[k])
        m1s[k, 0] = pair(k, x + 2, 0, hf).astype(BF16)
        remote(m1s.at[k, 0], m1r.at[k, 0], m1_ss.at[k, 0], m1_rs.at[k, 0], e, right).start()
        m1s[k, 1] = pair(k, x + 2, hf, hf).astype(BF16)
        remote(m1s.at[k, 1], m1r.at[k, 1], m1_ss.at[k, 1], m1_rs.at[k, 1], e, left).start()

    def reduce2(k):
        m2s[k, 0, :, hf:FL] = pair(k, x + 1, hf, hf).astype(BF16)
        m2s[k, 1, :, 0:hf] = pair(k, x - 1, 0, hf).astype(BF16)
        wait_recv(m1r.at[k, 0], m1_rs.at[k, 0])
        m2s[k, 0, :, 0:hf] = (pair(k, x + 1, 0, hf) + m1r[k, 0].astype(F32)).astype(BF16)
        remote(m2s.at[k, 0], m2r.at[k, 0], m2_ss.at[k, 0], m2_rs.at[k, 0], e, right).start()
        wait_recv(m1r.at[k, 1], m1_rs.at[k, 1])
        m2s[k, 1, :, hf:FL] = (pair(k, x - 1, hf, hf) + m1r[k, 1].astype(F32)).astype(BF16)
        remote(m2s.at[k, 1], m2r.at[k, 1], m2_ss.at[k, 1], m2_rs.at[k, 1], e, left).start()

    def reduce3(k):
        here = rows_of(k)
        wait_recv(sc_recv.at[k, pl.ds(0, HEAD - 1)], sc_rs.at[k])
        total = sc_recv[k, 0]
        for i in range(1, HEAD):
            total = total + sc_recv[k, i]
        column = jnp.sum(jnp.where(eye, total, 0.0), axis=1, keepdims=True)
        ret_send[here, FL:RET] = jnp.broadcast_to(column, (CH, 128)).astype(BF16)
        wait_recv(m2r.at[k, 0], m2_rs.at[k, 0])
        wait_recv(m2r.at[k, 1], m2_rs.at[k, 1])
        done = pair(k, x, 0, FL) + m2r[k, 0].astype(F32) + m2r[k, 1].astype(F32)
        ret_send[here, 0:FL] = done.astype(BF16)

        def one(j, carry):
            p = k * NZ + j
            remote(
                ret_send.at[block(p)], ret_recv.at[block(p)], r_ss.at[0], r_rs.at[k],
                exp_of(z + j, y + k), h,
            ).start()
            return carry

        lax.fori_loop(1 if k == 0 else 0, NZ, one, 0)
        if k == 0:
            ret_recv[0:CAP, :] = ret_send[0:CAP, :]

    def weights_down():
        def step(hh, carry):
            gdn[:, features(hh)] = tn(scaled[...], rows[hh, :, FL:XD]).astype(BF16)
            return carry

        lax.fori_loop(0, HEAD, step, 0)
        pltpu.make_async_copy(gdn, gdn_out.at[0], o_sem.at[1]).start()

    def weights_up():
        def step(hh, carry):
            gup[features(hh), :] = tn(rows[hh, :, 0:FL], delta[...]).astype(BF16)
            return carry

        lax.fori_loop(0, HEAD, step, 0)
        pltpu.make_async_copy(gup, gup_out.at[0], o_sem.at[0]).start()

    gather1(0)
    gather1(1)
    gather2(0)
    gather1(2)
    gather2(1)
    gather3(0)
    gather1(3)
    gather2(2)
    gather3(1)
    gather4(0)
    load_up.wait()
    load_dn.wait()
    compute(0)
    gather2(3)
    gather3(2)
    reduce1(0)
    gather4(1)
    compute(1)
    reduce2(0)
    gather3(3)
    reduce1(1)
    gather4(2)
    compute(2)
    reduce3(0)
    reduce2(1)
    reduce1(2)
    gather4(3)
    compute(3)
    reduce3(1)
    reduce2(2)
    reduce1(3)
    weights_down()
    reduce3(2)
    reduce2(3)
    weights_up()
    reduce3(3)

    back0 = jnp.zeros((TOK, RET), F32)
    back1 = jnp.zeros((TOK, RET), F32)
    for k in range(NCH):
        if k == 0:
            wait_recv(ret_recv.at[pl.ds(CAP, CH - CAP)], r_rs.at[k])
        else:
            wait_recv(ret_recv.at[rows_of(k)], r_rs.at[k])
        back0 = back0 + nn(pt0[:, rows_of(k)], ret_recv[rows_of(k), :])
        back1 = back1 + nn(pt1[:, rows_of(k)], ret_recv[rows_of(k), :])
    gt_out[...] = (back0[:, 0:FL] + back1[:, 0:FL]).astype(BF16)
    gg_out[:, 0:1] = back0[:, FL:FL + 1].astype(BF16)
    gg_out[:, 1:2] = back1[:, FL:FL + 1].astype(BF16)

    wait_send(send.at[pl.ds(CAP, ROWS - CAP)], d_send.at[0])
    whole = rows.at[0, :, pl.ds(0, XD)]
    wait_send(whole, ga_send.at[0])
    wait_send(whole, gb_send.at[0])
    for i in range(4):
        wait_send(whole, gs_send.at[i])
    halves = rows.at[0, pl.ds(0, ROWS // 2), pl.ds(0, XD)]
    wait_send(halves, a2_send.at[0])
    wait_send(halves, b2_send.at[0])
    for k in range(NCH):
        wait_send(sib_send.at[k], sib_ss.at[k])
        for i in range(2):
            wait_send(m1s.at[k, i], m1_ss.at[k, i])
            wait_send(m2s.at[k, i], m2_ss.at[k, i])
        wait_send(sc_recv.at[k, pl.ds(0, HEAD - 1)], sc_ss.at[k])
    wait_send(ret_send.at[pl.ds(CAP, ROWS - CAP)], r_ss.at[0])
    pltpu.make_async_copy(gdn, gdn_out.at[0], o_sem.at[1]).wait()
    pltpu.make_async_copy(gup, gup_out.at[0], o_sem.at[0]).wait()


def shards(tokens, cotangent, gates, expert_ids, w_up, w_down):
    vmem = pl.BlockSpec(memory_space=pltpu.VMEM)
    hbm = pl.BlockSpec(memory_space=pl.ANY)
    dma = pltpu.SemaphoreType.DMA
    return pl.pallas_call(
        kernel,
        out_shape=(
            jax.ShapeDtypeStruct((TOK, FL), BF16),
            jax.ShapeDtypeStruct((TOK, 2), BF16),
            jax.ShapeDtypeStruct((1, D, HID), BF16),
            jax.ShapeDtypeStruct((1, HID, D), BF16),
        ),
        in_specs=[vmem, vmem, vmem, vmem, hbm, hbm],
        out_specs=(vmem, vmem, hbm, hbm),
        scratch_shapes=[
            pltpu.VMEM((D, HID), BF16),
            pltpu.VMEM((HID, D), BF16),
            pltpu.VMEM((D, HID), BF16),
            pltpu.VMEM((HID, D), BF16),
            pltpu.VMEM((TOK, ROWS), BF16),
            pltpu.VMEM((TOK, ROWS), BF16),
            pltpu.VMEM((ROWS, MSG), BF16),
            pltpu.VMEM((HEAD, ROWS, MSG), BF16),
            pltpu.VMEM((ROWS, HID), BF16),
            pltpu.VMEM((ROWS, HID), BF16),
            pltpu.VMEM((NCH, NX, CH, FL), BF16),
            pltpu.VMEM((NCH, NX, CH, FL), BF16),
            pltpu.VMEM((NCH, NX, CH, FL), F32),
            pltpu.VMEM((NCH, 2, CH, FL // 2), BF16),
            pltpu.VMEM((NCH, 2, CH, FL // 2), BF16),
            pltpu.VMEM((NCH, 2, CH, FL), BF16),
            pltpu.VMEM((NCH, 2, CH, FL), BF16),
            pltpu.VMEM((NCH, 1, CH), F32),
            pltpu.VMEM((NCH, HEAD, 1, CH), F32),
            pltpu.VMEM((ROWS, RET), BF16),
            pltpu.VMEM((ROWS, RET), BF16),
            dma((2,)),
            dma((2,)),
            dma((1,)), dma((NCH,)),
            dma((1,)), dma((NCH,)),
            dma((1,)), dma((NCH,)),
            dma((1,)), dma((NCH,)),
            dma((1,)), dma((NCH,)),
            dma((4,)), dma((NCH, 4)),
            dma((NCH,)), dma((NCH,)),
            dma((NCH, 2)), dma((NCH, 2)),
            dma((NCH, 2)), dma((NCH, 2)),
            dma((NCH,)), dma((NCH,)),
            dma((1,)), dma((NCH,)),
        ],
        compiler_params=pltpu.CompilerParams(
            collective_id=0, has_side_effects=True, vmem_limit_bytes=56 * 1024 * 1024
        ),
        cost_estimate=pl.CostEstimate(
            flops=10 * ROWS * D * HID, bytes_accessed=8 * D * HID, transcendentals=2 * ROWS * HID
        ),
    )(tokens, cotangent, gates, expert_ids, w_up, w_down)


def solution(mesh):
    return jax.shard_map(
        shards,
        mesh=mesh,
        in_specs=(
            P("exp", "head"),
            P("exp", "head"),
            P("exp", None),
            P("exp", None),
            P("exp", None, "head"),
            P("exp", "head", None),
        ),
        out_specs=(
            P("exp", "head"),
            P("exp", None),
            P("exp", None, "head"),
            P("exp", "head", None),
        ),
        check_vma=False,
    )
```

```python
import math

import jax
import jax.numpy as jnp
from jax import lax
from jax.experimental import pallas as pl
from jax.experimental.pallas import tpu as pltpu
from jax.sharding import PartitionSpec as P

MESH = pl.DeviceIdType.MESH
BF16, F32, I32 = jnp.bfloat16, jnp.float32, jnp.int32

NZ, NY, NX = 8, 4, 4
EXP, HEAD = NZ * NY, 2 * NX
CAP = 16
TOK = 128
PER = 4
CH = PER * CAP
NCH = EXP // PER
ROWS = NCH * CH
FL = 512
HID = 256
D = HEAD * FL
XD = 2 * FL
MSG = XD + 128
RET = FL + 128


def offsets():
    order = []
    for reach, late in ((0, 0), (1, 0), (2, 0), (3, 0), (4, 0), (3, 1), (2, 1), (1, 1)):
        if reach in (0, NZ // 2):
            order += [(reach, 0), (reach, 1), (reach, NY - 1), (reach, 2)]
        elif late:
            order += [(reach, NY - 1), (NZ - reach, 1), (reach, 2), (NZ - reach, 2)]
        else:
            order += [(reach, 0), (NZ - reach, 0), (reach, 1), (NZ - reach, NY - 1)]
    return order


ORDER = offsets()


def gelu_parts(pre):
    phi = 0.5 * (1.0 + lax.erf(pre * math.sqrt(0.5)))
    act = pre * phi
    slope = phi + pre * jnp.exp(-0.5 * pre * pre) * (1.0 / math.sqrt(2.0 * math.pi))
    return act, slope


def nn(a, b):
    return jnp.dot(a, b, preferred_element_type=F32)


def nt(a, b):
    return lax.dot_general(a, b, (((1,), (1,)), ((), ())), preferred_element_type=F32)


def tn(a, b):
    return lax.dot_general(a, b, (((0,), (0,)), ((), ())), preferred_element_type=F32)


def kernel(
    tok_ref, cot_ref, gates_ref, ids_ref, wup_hbm, wdn_hbm,
    gt_out, gg_out, gup, gdn,
    wup, wdn, wup_t, wdn_t, pt0, pt1, send, rows, scaled, delta,
    sib_send, sib_recv, own, m1s, m1r, m2s, m2r, sc_send, sc_recv, ret_send, ret_recv,
    w_sem,
    d_send, d_recv, ga_send, ga_recv, gb_send, gb_recv, a2_send, a2_recv, b2_send, b2_recv,
    gs_send, gs_recv, sib_ss, sib_rs, m1_ss, m1_rs, m2_ss, m2_rs, sc_ss, sc_rs, r_ss, r_rs,
):
    e, h = lax.axis_index("exp"), lax.axis_index("head")
    z, y = e // NY, lax.rem(e, NY)
    x, c = h // 2, lax.rem(h, 2)

    def head_of(xx, cc):
        return lax.rem(xx + NX, NX) * 2 + cc

    right, left, opp = head_of(x + 1, c), head_of(x - 1, c), head_of(x + 2, c)
    sib = x * 2 + (1 - c)

    def exp_of(zz, yy):
        return lax.rem(zz + NZ, NZ) * NY + lax.rem(yy + NY, NY)

    barrier = pltpu.get_barrier_semaphore()

    def greet_exp(i, carry):
        pl.semaphore_signal(barrier, inc=1, device_id=(lax.rem(e + i, EXP), h), device_id_type=MESH)
        return carry

    def greet_head(i, carry):
        pl.semaphore_signal(barrier, inc=1, device_id=(e, lax.rem(h + i, HEAD)), device_id_type=MESH)
        return carry

    lax.fori_loop(1, EXP, greet_exp, 0)
    lax.fori_loop(1, HEAD, greet_head, 0)

    load_up = pltpu.make_async_copy(wup_hbm.at[0], wup, w_sem.at[0])
    load_dn = pltpu.make_async_copy(wdn_hbm.at[0], wdn, w_sem.at[1])
    load_up.start()
    load_dn.start()

    lane = lax.broadcasted_iota(I32, (TOK, 128), 1)
    sub = lax.broadcasted_iota(I32, (TOK, 128), 0)

    def column(ref, k):
        line = ref[k:k + 1, :].astype(F32)
        return jnp.sum(jnp.where(lane == sub, line, 0.0), axis=1, keepdims=True)

    def offset_of(expert):
        return ((z - (expert >> 2)) & (NZ - 1)) * NY + ((y - (expert & (NY - 1))) & (NY - 1))

    r0, r1 = offset_of(column(ids_ref, 0).astype(I32)), offset_of(column(ids_ref, 1).astype(I32))
    first = jnp.zeros((1, 128), F32)
    for p, (dz, dy) in enumerate(ORDER):
        first = jnp.where(lane[0:1] == dz * NY + dy, float(p * CAP), first)
    oh0, oh1 = r0 == lane, r1 == lane
    both = (oh0 | oh1).astype(BF16)
    place = nn((lane < sub).astype(BF16), both) + first
    d0 = jnp.sum(jnp.where(oh0, place, 0.0), axis=1, keepdims=True).astype(I32)
    d1 = jnp.sum(jnp.where(oh1, place, 0.0), axis=1, keepdims=True).astype(I32)
    slots = lax.broadcasted_iota(I32, (TOK, ROWS), 1)
    pt0[...] = (d0 == slots).astype(BF16)
    pt1[...] = (d1 == slots).astype(BF16)
    gate0 = jnp.broadcast_to(column(gates_ref, 0), (TOK, 128)).astype(BF16)
    gate1 = jnp.broadcast_to(column(gates_ref, 1), (TOK, 128)).astype(BF16)

    def rows_of(k):
        return pl.ds(k * CH, CH)

    def block(p):
        return pl.ds(p * CAP, CAP)

    def fill(k):
        here = rows_of(k)
        p0, p1 = pt0[:, here], pt1[:, here]
        both = p0 + p1
        send[here, 0:FL] = tn(both, tok_ref[...]).astype(BF16)
        send[here, FL:XD] = tn(both, cot_ref[...]).astype(BF16)
        send[here, XD:MSG] = (tn(p0, gate0) + tn(p1, gate1)).astype(BF16)

    def remote(src, dst, ss, rs, exp_i, head_i):
        return pltpu.make_async_remote_copy(
            src_ref=src, dst_ref=dst, send_sem=ss, recv_sem=rs,
            device_id=(exp_i, head_i), device_id_type=MESH,
        )

    def dispatch(k):
        for p in range(max(k * PER, 1), (k + 1) * PER):
            dz, dy = ORDER[p]
            remote(
                send.at[block(p)], rows.at[h, block(p)], d_send.at[0], d_recv.at[k],
                exp_of(z - dz, y - dy), h,
            ).start()

    def wait_recv(ref, rs):
        remote(ref, ref, rs, rs, e, sib).wait_recv()

    def wait_send(ref, ss):
        remote(ref, ref, ss, ss, e, sib).wait_send()

    fill(0)
    pl.semaphore_wait(barrier, EXP - 1 + HEAD - 1)
    dispatch(0)
    rows[h, 0:CAP, :] = send[0:CAP, :]
    for k in range(1, NCH):
        fill(k)
        dispatch(k)
    load_up.wait()
    load_dn.wait()
    for hh in range(HEAD):
        part_of = pl.ds(hh * FL, FL)
        wup_t[:, part_of] = wup[part_of, :].T
        wdn_t[part_of, :] = wdn[:, part_of].T

    def part(hh, k, start=0, size=CH):
        return rows.at[hh, pl.ds(k * CH + start, size), pl.ds(0, XD)]

    half = CH // 2

    def gather1(k):
        if k == 0:
            wait_recv(rows.at[h, pl.ds(CAP, CH - CAP)], d_recv.at[k])
        else:
            wait_recv(rows.at[h, rows_of(k)], d_recv.at[k])
        mine = part(h, k)
        remote(mine, mine, ga_send.at[0], ga_recv.at[k], e, right).start()
        remote(mine, mine, gb_send.at[0], gb_recv.at[k], e, left).start()
        remote(mine, mine, gs_send.at[0], gs_recv.at[k, 0], e, sib).start()

    def gather2(k):
        low, high = part(left, k, 0, half), part(right, k, half, half)
        wait_recv(part(left, k), ga_recv.at[k])
        remote(low, low, a2_send.at[0], a2_recv.at[k], e, right).start()
        remote(part(left, k), part(left, k), gs_send.at[1], gs_recv.at[k, 1], e, sib).start()
        wait_recv(part(right, k), gb_recv.at[k])
        remote(high, high, b2_send.at[0], b2_recv.at[k], e, left).start()
        remote(part(right, k), part(right, k), gs_send.at[2], gs_recv.at[k, 2], e, sib).start()

    def gather3(k):
        wait_recv(part(opp, k, 0, half), a2_recv.at[k])
        wait_recv(part(opp, k, half, half), b2_recv.at[k])
        remote(part(opp, k), part(opp, k), gs_send.at[3], gs_recv.at[k, 3], e, sib).start()

    def gather4(k):
        for i in range(4):
            wait_recv(part(h, k), gs_recv.at[k, i])

    eye = lane[0:CH] == sub[0:CH]

    def features(hh):
        return pl.ds(pl.multiple_of(hh * FL, FL), FL)

    def compute(k):
        here = rows_of(k)

        pre = jnp.zeros((CH, HID), F32)
        back = jnp.zeros((CH, HID), F32)
        for hh in range(HEAD):
            part_of = pl.ds(hh * FL, FL)
            pre = pre + nn(rows[hh, here, 0:FL], wup[part_of, :])
            back = back + nn(rows[hh, here, FL:XD], wdn_t[part_of, :])
        g = rows[h, here, XD:MSG][:, 0:1].astype(F32)
        act, slope = gelu_parts(pre)
        score = jnp.sum(back * act, axis=1, keepdims=True)
        scaled[here, :] = (g * act).astype(BF16)
        delta[here, :] = (g * back * slope).astype(BF16)

        terms = delta[here, :]
        for xx in range(NX):
            sib_send[k, xx] = nn(terms, wup_t[:, features(xx * 2 + (1 - c))]).astype(BF16)
        remote(sib_send.at[k], sib_recv.at[k], sib_ss.at[k], sib_rs.at[k], e, sib).start()
        line = jnp.sum(jnp.where(eye, score, 0.0), axis=0, keepdims=True)
        sc_send[k] = line
        sc_recv[k, h] = line

        def tell(i, carry):
            remote(
                sc_send.at[k], sc_recv.at[k, h], sc_ss.at[k], sc_rs.at[k], e, lax.rem(h + i, HEAD)
            ).start()
            return carry

        lax.fori_loop(1, HEAD, tell, 0)

        for xx in range(NX):
            own[k, xx] = nn(terms, wup_t[:, features(xx * 2 + c)])

    def pair(k, xx, start, size):
        at = lax.rem(xx + NX, NX)
        cols = pl.ds(start, size)
        return own[k, at, :, cols] + sib_recv[k, at, :, cols].astype(F32)

    hf = FL // 2

    def reduce1(k):
        wait_recv(sib_recv.at[k], sib_rs.at[k])
        m1s[k, 0] = pair(k, x + 2, 0, hf).astype(BF16)
        remote(m1s.at[k, 0], m1r.at[k, 0], m1_ss.at[k, 0], m1_rs.at[k, 0], e, right).start()
        m1s[k, 1] = pair(k, x + 2, hf, hf).astype(BF16)
        remote(m1s.at[k, 1], m1r.at[k, 1], m1_ss.at[k, 1], m1_rs.at[k, 1], e, left).start()

    def reduce2(k):
        m2s[k, 0, :, hf:FL] = pair(k, x + 1, hf, hf).astype(BF16)
        m2s[k, 1, :, 0:hf] = pair(k, x - 1, 0, hf).astype(BF16)
        wait_recv(m1r.at[k, 0], m1_rs.at[k, 0])
        m2s[k, 0, :, 0:hf] = (pair(k, x + 1, 0, hf) + m1r[k, 0].astype(F32)).astype(BF16)
        remote(m2s.at[k, 0], m2r.at[k, 0], m2_ss.at[k, 0], m2_rs.at[k, 0], e, right).start()
        wait_recv(m1r.at[k, 1], m1_rs.at[k, 1])
        m2s[k, 1, :, hf:FL] = (pair(k, x - 1, hf, hf) + m1r[k, 1].astype(F32)).astype(BF16)
        remote(m2s.at[k, 1], m2r.at[k, 1], m2_ss.at[k, 1], m2_rs.at[k, 1], e, left).start()

    def reduce3(k):
        here = rows_of(k)
        wait_recv(sc_recv.at[k, pl.ds(0, HEAD - 1)], sc_rs.at[k])
        total = sc_recv[k, 0]
        for i in range(1, HEAD):
            total = total + sc_recv[k, i]
        total = jnp.sum(jnp.where(eye, total, 0.0), axis=1, keepdims=True)
        ret_send[here, FL:RET] = jnp.broadcast_to(total, (CH, 128)).astype(BF16)
        wait_recv(m2r.at[k, 0], m2_rs.at[k, 0])
        wait_recv(m2r.at[k, 1], m2_rs.at[k, 1])
        done = pair(k, x, 0, FL) + m2r[k, 0].astype(F32) + m2r[k, 1].astype(F32)
        ret_send[here, 0:FL] = done.astype(BF16)

        for p in range(max(k * PER, 1), (k + 1) * PER):
            dz, dy = ORDER[p]
            remote(
                ret_send.at[block(p)], ret_recv.at[block(p)], r_ss.at[0], r_rs.at[k],
                exp_of(z + dz, y + dy), h,
            ).start()
        if k == 0:
            ret_recv[0:CAP, :] = ret_send[0:CAP, :]

    def weights_down():
        flat = scaled[...].T
        for hh in range(HEAD):
            gdn[0, :, hh * FL:(hh + 1) * FL] = nn(flat, rows[hh, :, FL:XD]).astype(BF16)

    def weights_up():
        for hh in range(HEAD):
            gup[0, hh * FL:(hh + 1) * FL, :] = tn(rows[hh, :, 0:FL], delta[...]).astype(BF16)

    stages = (gather1, gather2, gather3, gather4, compute, reduce1, reduce2, reduce3)
    lags = (0, 1, 2, 3, 3, 4, 5, 6)
    for tick in range(NCH + lags[-1]):
        for stage, lag in zip(stages, lags):
            k = tick - lag
            if 0 <= k < NCH:
                stage(k)
                if k == NCH - 1 and stage is compute:
                    weights_down()
                if k == NCH - 1 and stage is reduce1:
                    weights_up()

    back0 = jnp.zeros((TOK, RET), F32)
    back1 = jnp.zeros((TOK, RET), F32)
    for k in range(NCH):
        if k == 0:
            wait_recv(ret_recv.at[pl.ds(CAP, CH - CAP)], r_rs.at[k])
        else:
            wait_recv(ret_recv.at[rows_of(k)], r_rs.at[k])
        back0 = back0 + nn(pt0[:, rows_of(k)], ret_recv[rows_of(k), :])
        back1 = back1 + nn(pt1[:, rows_of(k)], ret_recv[rows_of(k), :])
    gt_out[...] = (back0[:, 0:FL] + back1[:, 0:FL]).astype(BF16)
    for i, back in enumerate((back0, back1)):
        line = jnp.sum(jnp.where(lane == sub, back[:, FL:RET], 0.0), axis=0, keepdims=True)
        gg_out[i:i + 1, :] = line.astype(BF16)

    wait_send(send.at[pl.ds(CAP, ROWS - CAP)], d_send.at[0])
    whole = rows.at[0, :, pl.ds(0, XD)]
    wait_send(whole, ga_send.at[0])
    wait_send(whole, gb_send.at[0])
    for i in range(4):
        wait_send(whole, gs_send.at[i])
    halves = rows.at[0, pl.ds(0, ROWS // 2), pl.ds(0, XD)]
    wait_send(halves, a2_send.at[0])
    wait_send(halves, b2_send.at[0])
    for k in range(NCH):
        wait_send(sib_send.at[k], sib_ss.at[k])
        for i in range(2):
            wait_send(m1s.at[k, i], m1_ss.at[k, i])
            wait_send(m2s.at[k, i], m2_ss.at[k, i])
        wait_send(sc_recv.at[k, pl.ds(0, HEAD - 1)], sc_ss.at[k])
    wait_send(ret_send.at[pl.ds(CAP, ROWS - CAP)], r_ss.at[0])


def store(*refs):
    ins, outs, sem = refs[:4], refs[4:8], refs[8]
    copies = [pltpu.make_async_copy(ins[i], outs[i], sem.at[i]) for i in range(4)]
    for one in copies:
        one.start()
    for one in copies:
        one.wait()


def shards(tokens, cotangent, gates, expert_ids, w_up, w_down):
    vmem = pl.BlockSpec(memory_space=pltpu.VMEM)
    hbm = pl.BlockSpec(memory_space=pl.ANY)
    dma = pltpu.SemaphoreType.DMA
    shapes = ((TOK, FL), (2, TOK), (1, D, HID), (1, HID, D))
    results = pl.pallas_call(
        kernel,
        out_shape=tuple(pltpu.VMEM(shape, BF16) for shape in shapes),
        in_specs=[vmem, vmem, vmem, vmem, hbm, hbm],
        out_specs=(vmem, vmem, vmem, vmem),
        scratch_shapes=[
            pltpu.VMEM((D, HID), BF16),
            pltpu.VMEM((HID, D), BF16),
            pltpu.VMEM((HID, D), BF16),
            pltpu.VMEM((D, HID), BF16),
            pltpu.VMEM((TOK, ROWS), BF16),
            pltpu.VMEM((TOK, ROWS), BF16),
            pltpu.VMEM((ROWS, MSG), BF16),
            pltpu.VMEM((HEAD, ROWS, MSG), BF16),
            pltpu.VMEM((ROWS, HID), BF16),
            pltpu.VMEM((ROWS, HID), BF16),
            pltpu.VMEM((NCH, NX, CH, FL), BF16),
            pltpu.VMEM((NCH, NX, CH, FL), BF16),
            pltpu.VMEM((NCH, NX, CH, FL), F32),
            pltpu.VMEM((NCH, 2, CH, FL // 2), BF16),
            pltpu.VMEM((NCH, 2, CH, FL // 2), BF16),
            pltpu.VMEM((NCH, 2, CH, FL), BF16),
            pltpu.VMEM((NCH, 2, CH, FL), BF16),
            pltpu.VMEM((NCH, 1, 128), F32),
            pltpu.VMEM((NCH, HEAD, 1, 128), F32),
            pltpu.VMEM((ROWS, RET), BF16),
            pltpu.VMEM((ROWS, RET), BF16),
            dma((2,)),
            dma((1,)), dma((NCH,)),
            dma((1,)), dma((NCH,)),
            dma((1,)), dma((NCH,)),
            dma((1,)), dma((NCH,)),
            dma((1,)), dma((NCH,)),
            dma((4,)), dma((NCH, 4)),
            dma((NCH,)), dma((NCH,)),
            dma((NCH, 2)), dma((NCH, 2)),
            dma((NCH, 2)), dma((NCH, 2)),
            dma((NCH,)), dma((NCH,)),
            dma((1,)), dma((NCH,)),
        ],
        compiler_params=pltpu.CompilerParams(
            collective_id=0, has_side_effects=True, vmem_limit_bytes=56 * 1024 * 1024
        ),
        cost_estimate=pl.CostEstimate(
            flops=10 * ROWS * D * HID, bytes_accessed=8 * D * HID, transcendentals=2 * ROWS * HID
        ),
    )(tokens, cotangent, gates.T, expert_ids.T, w_up, w_down)
    grad_tokens, grad_gates, grad_up, grad_down = pl.pallas_call(
        store,
        out_shape=tuple(jax.ShapeDtypeStruct(shape, BF16) for shape in shapes),
        in_specs=[vmem] * 4,
        out_specs=(hbm,) * 4,
        scratch_shapes=[dma((4,))],
        compiler_params=pltpu.CompilerParams(vmem_limit_bytes=16 * 1024 * 1024),
    )(*results)
    return grad_tokens, grad_gates.T, grad_up, grad_down


def solution(mesh):
    return jax.shard_map(
        shards,
        mesh=mesh,
        in_specs=(
            P("exp", "head"),
            P("exp", "head"),
            P("exp", None),
            P("exp", None),
            P("exp", None, "head"),
            P("exp", "head", None),
        ),
        out_specs=(
            P("exp", "head"),
            P("exp", None),
            P("exp", None, "head"),
            P("exp", "head", None),
        ),
        check_vma=False,
    )
```

```python
import math

import jax
import jax.numpy as jnp
from jax import lax
from jax.experimental import pallas as pl
from jax.experimental.pallas import tpu as pltpu
from jax.sharding import PartitionSpec as P

MESH = pl.DeviceIdType.MESH
BF16, F32, I32 = jnp.bfloat16, jnp.float32, jnp.int32

NZ, NY, NX = 8, 4, 4
EXP, HEAD = NZ * NY, 2 * NX
CAP = 16
TOK = 128
PER = 4
CH = PER * CAP
NCH = EXP // PER
ROWS = NCH * CH
FL = 512
HID = 256
D = HEAD * FL
XD = 2 * FL
LINE = 128


def offsets():
    order = []
    for reach, late in ((0, 0), (2, 0), (3, 0), (4, 0), (1, 0), (3, 1), (2, 1), (1, 1)):
        if reach in (0, NZ // 2):
            order += [(reach, 0), (reach, 1), (reach, NY - 1), (reach, 2)]
        elif late:
            order += [(reach, NY - 1), (NZ - reach, 1), (reach, 2), (NZ - reach, 2)]
        else:
            order += [(reach, 0), (NZ - reach, 0), (reach, 1), (NZ - reach, NY - 1)]
    return order


ORDER = offsets()
NEAR = (0, 4, 7)
FAR = (1, 6, 3, 2, 5)
AHEAD = 3
PLAN = (
    ("g1", 1), ("d", 2), ("pass", 0), ("g1", 6), ("d", 5), ("g2", 1), ("near", 0), ("g2", 6),
    ("g1", 3), ("g3", 1), ("g3", 6), ("c", 1), ("g1", 2), ("g2", 3), ("near", 4), ("g3", 0),
    ("c", 6), ("r1", 1), ("g2", 2), ("g1", 5), ("near", 7), ("g3", 3), ("c", 0), ("r1", 6),
    ("r2", 1), ("g3", 2), ("c", 3), ("r1", 0), ("g2", 5), ("r2", 6), ("g3", 4), ("r3", 1),
    ("c", 2), ("r1", 3), ("r2", 0), ("g3", 5), ("r3", 6), ("c", 4), ("r1", 2), ("r2", 3),
    ("g3", 7), ("r3", 0), ("c", 5), ("r1", 4), ("r2", 2), ("r3", 3), ("c", 7), ("r1", 5),
    ("r2", 4), ("r3", 2), ("wd", 0), ("r1", 7), ("r2", 5), ("wu", 0), ("r3", 4), ("r2", 7),
    ("r3", 5), ("r3", 7),
)


def gelu_parts(pre):
    phi = 0.5 * (1.0 + lax.erf(pre * math.sqrt(0.5)))
    act = pre * phi
    slope = phi + pre * jnp.exp(-0.5 * pre * pre) * (1.0 / math.sqrt(2.0 * math.pi))
    return act, slope


def nn(a, b):
    return jnp.dot(a, b, preferred_element_type=F32)


def nt(a, b):
    return lax.dot_general(a, b, (((1,), (1,)), ((), ())), preferred_element_type=F32)


def tn(a, b):
    return lax.dot_general(a, b, (((0,), (0,)), ((), ())), preferred_element_type=F32)


def kernel(
    tok_ref, cot_ref, gates_ref, ids_ref, wup_hbm, wdn_hbm,
    gt_out, gg_out, gup, gdn,
    wup, wdn, wup_t, wdn_t, pt0, pt1, raw, send, near, rows, gate_lines, gate_in, score_lines, score_in, scaled, delta,
    sib_send, sib_recv, own, m1s, m1r, m2s, m2r, sc_send, sc_recv, ret_send, ret_recv,
    w_sem,
    t_send, t_recv, n_send, n_recv, d_send, d_recv, gl_send, gl_recv, sl_send, sl_recv, ga_send, ga_recv, gb_send, gb_recv, a2_send, a2_recv, b2_send, b2_recv,
    gs_send, gs_recv, sib_ss, sib_rs, m1_ss, m1_rs, m2_ss, m2_rs, sc_ss, sc_rs, r_ss, r_rs,
):
    e, h = lax.axis_index("exp"), lax.axis_index("head")
    z, y = e // NY, lax.rem(e, NY)
    x, c = h // 2, lax.rem(h, 2)

    def head_of(xx, cc):
        return lax.rem(xx + NX, NX) * 2 + cc

    xr, xl, xo = lax.rem(x + 1, NX), lax.rem(x + NX - 1, NX), lax.rem(x + 2, NX)
    right, left = head_of(x + 1, c), head_of(x - 1, c)
    sib = x * 2 + (1 - c)

    def exp_of(zz, yy):
        return lax.rem(zz + NZ, NZ) * NY + lax.rem(yy + NY, NY)

    barrier = pltpu.get_barrier_semaphore()

    def greet_exp(i, carry):
        pl.semaphore_signal(barrier, inc=1, device_id=(lax.rem(e + i, EXP), h), device_id_type=MESH)
        return carry

    def greet_head(i, carry):
        pl.semaphore_signal(barrier, inc=1, device_id=(e, lax.rem(h + i, HEAD)), device_id_type=MESH)
        return carry

    lax.fori_loop(1, EXP, greet_exp, 0)
    lax.fori_loop(1, HEAD, greet_head, 0)

    load_up = pltpu.make_async_copy(wup_hbm.at[0], wup, w_sem.at[0])
    load_dn = pltpu.make_async_copy(wdn_hbm.at[0], wdn, w_sem.at[1])
    load_up.start()
    load_dn.start()

    lane = lax.broadcasted_iota(I32, (TOK, 128), 1)
    sub = lax.broadcasted_iota(I32, (TOK, 128), 0)

    def column(ref, k):
        line = ref[k:k + 1, :].astype(F32)
        return jnp.sum(jnp.where(lane == sub, line, 0.0), axis=1, keepdims=True)

    def offset_of(expert):
        return ((z - (expert >> 2)) & (NZ - 1)) * NY + ((y - (expert & (NY - 1))) & (NY - 1))

    r0, r1 = offset_of(column(ids_ref, 0).astype(I32)), offset_of(column(ids_ref, 1).astype(I32))
    first = jnp.zeros((1, 128), F32)
    for p, (dz, dy) in enumerate(ORDER):
        first = jnp.where(lane[0:1] == dz * NY + dy, float(p * CAP), first)
    oh0, oh1 = r0 == lane, r1 == lane
    both = (oh0 | oh1).astype(BF16)
    place = nn((lane < sub).astype(BF16), both) + first
    d0 = jnp.sum(jnp.where(oh0, place, 0.0), axis=1, keepdims=True).astype(I32)
    d1 = jnp.sum(jnp.where(oh1, place, 0.0), axis=1, keepdims=True).astype(I32)
    slots = lax.broadcasted_iota(I32, (TOK, ROWS), 1)
    pt0[...] = (d0 == slots).astype(BF16)
    pt1[...] = (d1 == slots).astype(BF16)
    gates = [jnp.broadcast_to(gates_ref[k:k + 1, :], (16, TOK)) for k in range(2)]
    gate_row = (nn(gates[0], pt0[...]) + nn(gates[1], pt1[...]))[0:1, :]
    for i in range(ROWS // LINE):
        gate_lines[i] = gate_row[:, i * LINE:(i + 1) * LINE]
    gate_in[0] = gate_lines[0]
    slot_of = lax.broadcasted_iota(I32, (1, LINE), 1) // CAP

    def merge(ref, first, count):
        line = jnp.zeros((1, LINE), F32)
        for p in range(first, first + count):
            line = jnp.where(slot_of == p % 8, ref[p], line)
        return line

    def rows_of(k):
        return pl.ds(k * CH, CH)

    def block(p):
        return pl.ds(p * CAP, CAP)

    def fill(k):
        here = rows_of(k)
        p0, p1 = pt0[:, here], pt1[:, here]
        send[here, :] = tn(p0 + p1, raw[x]).astype(BF16)

    def fill_near(k):
        here, there = rows_of(k), rows_of(NEAR.index(k))
        p0, p1 = pt0[:, here], pt1[:, here]
        for xx in range(NX):
            near[xx, there, :] = tn(p0 + p1, raw[xx]).astype(BF16)

    def remote(src, dst, ss, rs, exp_i, head_i):
        return pltpu.make_async_remote_copy(
            src_ref=src, dst_ref=dst, send_sem=ss, recv_sem=rs,
            device_id=(exp_i, head_i), device_id_type=MESH,
        )

    def send_gates(k):
        for p in range(max(k * PER, 1), (k + 1) * PER):
            dz, dy = ORDER[p]
            remote(
                gate_lines.at[p // 8], gate_in.at[p], gl_send.at[0], gl_recv.at[k], exp_of(z - dz, y - dy), h
            ).start()

    def dispatch(k):
        for p in range(k * PER, (k + 1) * PER):
            dz, dy = ORDER[p]
            remote(
                send.at[block(p)], rows.at[c, x, block(p)], d_send.at[0], d_recv.at[k],
                exp_of(z - dz, y - dy), h,
            ).start()

    def dispatch_near(k):
        for p in range(max(k * PER, 1), (k + 1) * PER):
            dz, dy = ORDER[p]
            remote(
                near.at[:, block(p + (NEAR.index(k) - k) * PER)], rows.at[c, :, block(p)],
                n_send.at[0], n_recv.at[k], exp_of(z - dz, y - dy), h,
            ).start()

    def wait_recv(ref, rs):
        remote(ref, ref, rs, rs, e, sib).wait_recv()

    def wait_send(ref, ss):
        remote(ref, ref, ss, ss, e, sib).wait_send()

    raw[x, :, 0:FL] = tok_ref[...]
    raw[x, :, FL:XD] = cot_ref[...]
    fill(FAR[0])
    pl.semaphore_wait(barrier, EXP - 1 + HEAD - 1)
    mine = raw.at[x]
    remote(mine, mine, t_send.at[0], t_recv.at[0], e, right).start()
    remote(mine, mine, t_send.at[1], t_recv.at[1], e, left).start()
    dispatch(FAR[0])
    for k in FAR[1:AHEAD]:
        fill(k)
        dispatch(k)
    for k in FAR[AHEAD:]:
        fill(k)
    for k in range(NCH):
        send_gates(k)
    load_up.wait()
    load_dn.wait()
    for hh in range(HEAD):
        part_of = pl.ds(hh * FL, FL)
        wup_t[:, part_of] = wup[part_of, :].T
        wdn_t[part_of, :] = wdn[:, part_of].T

    def pass_raw(k):
        low, high = raw.at[xl, pl.ds(0, TOK // 2)], raw.at[xr, pl.ds(TOK // 2, TOK // 2)]
        wait_recv(raw.at[xl], t_recv.at[0])
        remote(low, low, t_send.at[2], t_recv.at[2], e, right).start()
        wait_recv(raw.at[xr], t_recv.at[1])
        remote(high, high, t_send.at[3], t_recv.at[3], e, left).start()

    def send_near(k):
        if k == NEAR[0]:
            wait_recv(raw.at[xo, pl.ds(0, TOK // 2)], t_recv.at[2])
            wait_recv(raw.at[xo, pl.ds(TOK // 2, TOK // 2)], t_recv.at[3])
        fill_near(k)
        dispatch_near(k)
        if k == 0:
            rows[c, :, 0:CAP, :] = near[:, 0:CAP, :]

    def part(xx, k, start=0, size=CH):
        return rows.at[c, xx, pl.ds(k * CH + start, size)]

    def whole(cc, k, start=0):
        return rows.at[cc, :, pl.ds(k * CH + start, CH - start)]

    half = CH // 2

    def gather1(k):
        if k in FAR:
            wait_recv(rows.at[c, x, rows_of(k)], d_recv.at[k])
            mine = part(x, k)
            remote(mine, mine, ga_send.at[0], ga_recv.at[k], e, right).start()
            remote(mine, mine, gb_send.at[0], gb_recv.at[k], e, left).start()
            remote(mine, mine, gs_send.at[0], gs_recv.at[k, 0], e, sib).start()

    def gather2(k):
        if k in FAR:
            low, high = part(xl, k, 0, half), part(xr, k, half, half)
            wait_recv(part(xl, k), ga_recv.at[k])
            remote(low, low, a2_send.at[0], a2_recv.at[k], e, right).start()
            remote(part(xl, k), part(xl, k), gs_send.at[1], gs_recv.at[k, 1], e, sib).start()
            wait_recv(part(xr, k), gb_recv.at[k])
            remote(high, high, b2_send.at[0], b2_recv.at[k], e, left).start()
            remote(part(xr, k), part(xr, k), gs_send.at[2], gs_recv.at[k, 2], e, sib).start()

    def gather3(k):
        if k in FAR:
            wait_recv(part(xo, k, 0, half), a2_recv.at[k])
            wait_recv(part(xo, k, half, half), b2_recv.at[k])
            remote(part(xo, k), part(xo, k), gs_send.at[3], gs_recv.at[k, 3], e, sib).start()
        else:
            start = CAP if k == 0 else 0
            wait_recv(whole(c, k, start), n_recv.at[k])
            remote(whole(c, k), whole(c, k), gs_send.at[4], gs_recv.at[k, 0], e, sib).start()

    def gather4(k):
        if k in FAR:
            for i in range(4):
                wait_recv(part(x, k), gs_recv.at[k, i])
        else:
            wait_recv(whole(1 - c, k), gs_recv.at[k, 0])

    def eye(k):
        return lane[0:CH] == sub[0:CH] + k % 2 * CH

    def features(hh):
        return pl.ds(pl.multiple_of(hh * FL, FL), FL)

    def compute(k):
        gather4(k)
        here = rows_of(k)

        pre = jnp.zeros((CH, HID), F32)
        back = jnp.zeros((CH, HID), F32)
        for hh in range(HEAD):
            part_of = pl.ds(hh * FL, FL)
            pre = pre + nn(rows[hh % 2, hh // 2, here, 0:FL], wup[part_of, :])
            back = back + nn(rows[hh % 2, hh // 2, here, FL:XD], wdn_t[part_of, :])
        first = 1 if k == 0 else 0
        wait_recv(gate_in.at[pl.ds(k * PER + first, PER - first)], gl_recv.at[k])
        g = jnp.sum(jnp.where(eye(k), merge(gate_in, k * PER, PER), 0.0), axis=1, keepdims=True)
        act, slope = gelu_parts(pre)
        score = jnp.sum(back * act, axis=1, keepdims=True)
        scaled[here, :] = (g * act).astype(BF16)
        delta[here, :] = (g * back * slope).astype(BF16)

        terms = delta[here, :]
        for xx in range(NX):
            sib_send[k, xx] = nn(terms, wup_t[:, features(xx * 2 + (1 - c))]).astype(BF16)
        remote(sib_send.at[k], sib_recv.at[k], sib_ss.at[k], sib_rs.at[k], e, sib).start()
        line = jnp.sum(jnp.where(eye(k), score, 0.0), axis=0, keepdims=True)
        sc_send[k] = line
        sc_recv[k, h] = line

        def tell(i, carry):
            remote(
                sc_send.at[k], sc_recv.at[k, h], sc_ss.at[k], sc_rs.at[k], e, lax.rem(h + i, HEAD)
            ).start()
            return carry

        lax.fori_loop(1, HEAD, tell, 0)

        for xx in range(NX):
            own[k, xx] = nn(terms, wup_t[:, features(xx * 2 + c)])

    def pair(k, xx, start, size):
        at = lax.rem(xx + NX, NX)
        cols = pl.ds(start, size)
        return own[k, at, :, cols] + sib_recv[k, at, :, cols].astype(F32)

    hf = FL // 2

    def reduce1(k):
        wait_recv(sib_recv.at[k], sib_rs.at[k])
        m1s[k, 0] = pair(k, x + 2, 0, hf).astype(BF16)
        remote(m1s.at[k, 0], m1r.at[k, 0], m1_ss.at[k, 0], m1_rs.at[k, 0], e, right).start()
        m1s[k, 1] = pair(k, x + 2, hf, hf).astype(BF16)
        remote(m1s.at[k, 1], m1r.at[k, 1], m1_ss.at[k, 1], m1_rs.at[k, 1], e, left).start()

    def reduce2(k):
        m2s[k, 0, :, hf:FL] = pair(k, x + 1, hf, hf).astype(BF16)
        m2s[k, 1, :, 0:hf] = pair(k, x - 1, 0, hf).astype(BF16)
        wait_recv(m1r.at[k, 0], m1_rs.at[k, 0])
        m2s[k, 0, :, 0:hf] = (pair(k, x + 1, 0, hf) + m1r[k, 0].astype(F32)).astype(BF16)
        remote(m2s.at[k, 0], m2r.at[k, 0], m2_ss.at[k, 0], m2_rs.at[k, 0], e, right).start()
        wait_recv(m1r.at[k, 1], m1_rs.at[k, 1])
        m2s[k, 1, :, hf:FL] = (pair(k, x - 1, hf, hf) + m1r[k, 1].astype(F32)).astype(BF16)
        remote(m2s.at[k, 1], m2r.at[k, 1], m2_ss.at[k, 1], m2_rs.at[k, 1], e, left).start()

    def reduce3(k):
        here = rows_of(k)
        wait_recv(sc_recv.at[k, pl.ds(0, HEAD - 1)], sc_rs.at[k])
        total = sc_recv[k, 0]
        for i in range(1, HEAD):
            total = total + sc_recv[k, i]
        score_lines[k] = total.astype(BF16).astype(F32)
        wait_recv(m2r.at[k, 0], m2_rs.at[k, 0])
        wait_recv(m2r.at[k, 1], m2_rs.at[k, 1])
        done = pair(k, x, 0, FL) + m2r[k, 0].astype(F32) + m2r[k, 1].astype(F32)
        ret_send[here, :] = done.astype(BF16)

        for p in range(max(k * PER, 1), (k + 1) * PER):
            dz, dy = ORDER[p]
            to = exp_of(z + dz, y + dy)
            remote(
                ret_send.at[block(p)], ret_recv.at[block(p)], r_ss.at[0], r_rs.at[k], to, h
            ).start()
            remote(
                score_lines.at[k], score_in.at[p], sl_send.at[0], sl_recv.at[0], to, h
            ).start()
        if k == 0:
            ret_recv[0:CAP, :] = ret_send[0:CAP, :]
            score_in[0] = score_lines[0]

    def weights_down(k):
        flat = scaled[...].T
        for hh in range(HEAD):
            gdn[0, :, hh * FL:(hh + 1) * FL] = nn(flat, rows[hh % 2, hh // 2, :, FL:XD]).astype(BF16)

    def weights_up(k):
        for hh in range(HEAD):
            gup[0, hh * FL:(hh + 1) * FL, :] = tn(rows[hh % 2, hh // 2, :, 0:FL], delta[...]).astype(BF16)

    stages = {
        "pass": pass_raw, "d": dispatch, "near": send_near, "g1": gather1, "g2": gather2, "g3": gather3,
        "c": compute, "r1": reduce1, "r2": reduce2, "r3": reduce3, "wd": weights_down, "wu": weights_up,
    }
    for stage, k in PLAN:
        stages[stage](k)

    total = jnp.zeros((TOK, FL), F32)
    for k in range(NCH):
        here = rows_of(k)
        if k == 0:
            wait_recv(ret_recv.at[pl.ds(CAP, CH - CAP)], r_rs.at[k])
        else:
            wait_recv(ret_recv.at[here], r_rs.at[k])
        total = total + nn(pt0[:, here] + pt1[:, here], ret_recv[here, :])
    gt_out[...] = total.astype(BF16)
    wait_recv(score_in.at[pl.ds(1, EXP - 1)], sl_recv.at[0])
    for k, pt in enumerate((pt0, pt1)):
        picked = jnp.zeros((TOK, LINE), F32)
        for i in range(ROWS // LINE):
            picked = picked + pt[:, i * LINE:(i + 1) * LINE].astype(F32) * merge(score_in, i * 8, 8)
        score = jnp.sum(picked, axis=1, keepdims=True)
        gg_out[k:k + 1, :] = jnp.sum(jnp.where(lane == sub, score, 0.0), axis=0, keepdims=True).astype(BF16)

    wait_send(raw.at[0], t_send.at[0])
    wait_send(raw.at[0], t_send.at[1])
    wait_send(raw.at[0, pl.ds(0, TOK // 2)], t_send.at[2])
    wait_send(raw.at[0, pl.ds(0, TOK // 2)], t_send.at[3])
    far_rows, near_rows = len(FAR) * CH, len(NEAR) * CH
    wait_send(send.at[pl.ds(0, far_rows)], d_send.at[0])
    wait_send(near.at[:, pl.ds(CAP, near_rows - CAP)], n_send.at[0])
    wait_send(gate_in.at[pl.ds(1, EXP - 1)], gl_send.at[0])
    wait_send(score_in.at[pl.ds(1, EXP - 1)], sl_send.at[0])
    gathered = rows.at[0, 0, pl.ds(0, far_rows)]
    wait_send(gathered, ga_send.at[0])
    wait_send(gathered, gb_send.at[0])
    for i in range(4):
        wait_send(gathered, gs_send.at[i])
    wait_send(rows.at[0, :, pl.ds(0, near_rows)], gs_send.at[4])
    halves = rows.at[0, 0, pl.ds(0, far_rows // 2)]
    wait_send(halves, a2_send.at[0])
    wait_send(halves, b2_send.at[0])
    for k in range(NCH):
        wait_send(sib_send.at[k], sib_ss.at[k])
        for i in range(2):
            wait_send(m1s.at[k, i], m1_ss.at[k, i])
            wait_send(m2s.at[k, i], m2_ss.at[k, i])
        wait_send(sc_recv.at[k, pl.ds(0, HEAD - 1)], sc_ss.at[k])
    wait_send(ret_send.at[pl.ds(CAP, ROWS - CAP)], r_ss.at[0])


def store(*refs):
    ins, outs, sem = refs[:4], refs[4:8], refs[8]
    copies = [pltpu.make_async_copy(ins[i], outs[i], sem.at[i]) for i in range(4)]
    for one in copies:
        one.start()
    for one in copies:
        one.wait()


def shards(tokens, cotangent, gates, expert_ids, w_up, w_down):
    vmem = pl.BlockSpec(memory_space=pltpu.VMEM)
    hbm = pl.BlockSpec(memory_space=pl.ANY)
    dma = pltpu.SemaphoreType.DMA
    shapes = ((TOK, FL), (2, TOK), (1, D, HID), (1, HID, D))
    results = pl.pallas_call(
        kernel,
        out_shape=tuple(pltpu.VMEM(shape, BF16) for shape in shapes),
        in_specs=[vmem, vmem, vmem, vmem, hbm, hbm],
        out_specs=(vmem, vmem, vmem, vmem),
        scratch_shapes=[
            pltpu.VMEM((D, HID), BF16),
            pltpu.VMEM((HID, D), BF16),
            pltpu.VMEM((HID, D), BF16),
            pltpu.VMEM((D, HID), BF16),
            pltpu.VMEM((TOK, ROWS), BF16),
            pltpu.VMEM((TOK, ROWS), BF16),
            pltpu.VMEM((NX, TOK, XD), BF16),
            pltpu.VMEM((ROWS, XD), BF16),
            pltpu.VMEM((NX, len(NEAR) * CH, XD), BF16),
            pltpu.VMEM((2, NX, ROWS, XD), BF16),
            pltpu.VMEM((ROWS // LINE, 1, LINE), F32),
            pltpu.VMEM((EXP, 1, LINE), F32),
            pltpu.VMEM((NCH, 1, LINE), F32),
            pltpu.VMEM((EXP, 1, LINE), F32),
            pltpu.VMEM((ROWS, HID), BF16),
            pltpu.VMEM((ROWS, HID), BF16),
            pltpu.VMEM((NCH, NX, CH, FL), BF16),
            pltpu.VMEM((NCH, NX, CH, FL), BF16),
            pltpu.VMEM((NCH, NX, CH, FL), F32),
            pltpu.VMEM((NCH, 2, CH, FL // 2), BF16),
            pltpu.VMEM((NCH, 2, CH, FL // 2), BF16),
            pltpu.VMEM((NCH, 2, CH, FL), BF16),
            pltpu.VMEM((NCH, 2, CH, FL), BF16),
            pltpu.VMEM((NCH, 1, LINE), F32),
            pltpu.VMEM((NCH, HEAD, 1, LINE), F32),
            pltpu.VMEM((ROWS, FL), BF16),
            pltpu.VMEM((ROWS, FL), BF16),
            dma((2,)),
            dma((4,)), dma((4,)),
            dma((1,)), dma((NCH,)),
            dma((1,)), dma((NCH,)),
            dma((1,)), dma((NCH,)),
            dma((1,)), dma((1,)),
            dma((1,)), dma((NCH,)),
            dma((1,)), dma((NCH,)),
            dma((1,)), dma((NCH,)),
            dma((1,)), dma((NCH,)),
            dma((5,)), dma((NCH, 4)),
            dma((NCH,)), dma((NCH,)),
            dma((NCH, 2)), dma((NCH, 2)),
            dma((NCH, 2)), dma((NCH, 2)),
            dma((NCH,)), dma((NCH,)),
            dma((1,)), dma((NCH,)),
        ],
        compiler_params=pltpu.CompilerParams(
            collective_id=0, has_side_effects=True, vmem_limit_bytes=56 * 1024 * 1024
        ),
        cost_estimate=pl.CostEstimate(
            flops=10 * ROWS * D * HID, bytes_accessed=8 * D * HID, transcendentals=2 * ROWS * HID
        ),
    )(tokens, cotangent, gates.T, expert_ids.T, w_up, w_down)
    grad_tokens, grad_gates, grad_up, grad_down = pl.pallas_call(
        store,
        out_shape=tuple(jax.ShapeDtypeStruct(shape, BF16) for shape in shapes),
        in_specs=[vmem] * 4,
        out_specs=(hbm,) * 4,
        scratch_shapes=[dma((4,))],
        compiler_params=pltpu.CompilerParams(vmem_limit_bytes=16 * 1024 * 1024),
    )(*results)
    return grad_tokens, grad_gates.T, grad_up, grad_down


def solution(mesh):
    return jax.shard_map(
        shards,
        mesh=mesh,
        in_specs=(
            P("exp", "head"),
            P("exp", "head"),
            P("exp", None),
            P("exp", None),
            P("exp", None, "head"),
            P("exp", "head", None),
        ),
        out_specs=(
            P("exp", "head"),
            P("exp", None),
            P("exp", None, "head"),
            P("exp", "head", None),
        ),
        check_vma=False,
    )
```

```python
import math

import jax
import jax.numpy as jnp
from jax import lax
from jax.experimental import pallas as pl
from jax.experimental.pallas import tpu as pltpu
from jax.sharding import PartitionSpec as P

MESH = pl.DeviceIdType.MESH
BF16, F32, I32 = jnp.bfloat16, jnp.float32, jnp.int32

NZ, NY, NX = 8, 4, 4
EXP, HEAD = NZ * NY, 2 * NX
CAP = 16
TOK = 128
PER = 4
CH = PER * CAP
NCH = EXP // PER
ROWS = NCH * CH
FL = 512
HID = 256
D = HEAD * FL
XD = 2 * FL
LINE = 128


def offsets():
    order = []
    for reach, late in ((2, 0), (3, 0), (0, 0), (3, 1), (4, 0), (1, 0), (2, 1), (1, 1)):
        if reach in (0, NZ // 2):
            order += [(reach, 0), (reach, 1), (reach, NY - 1), (reach, 2)]
        elif late:
            order += [(reach, NY - 1), (NZ - reach, 1), (reach, 2), (NZ - reach, 2)]
        else:
            order += [(reach, 0), (NZ - reach, 0), (reach, 1), (NZ - reach, NY - 1)]
    return order


ORDER = offsets()
HOME = 2
NEAR = (HOME, 5, 7)
FAR = (0, 1, 3, 4, 6)
AHEAD = 3
GROUPS = ((0, 1), (1, 1), (2, 1), (3, 1), (4, 1), (5, 1), (6, 1), (7, 1))
PLAN = (
    ("g1", 0), ("d", 4), ("pass", 0), ("g2", 0), ("g1", 1), ("d", 6), ("near", 2), ("g3", 0),
    ("g1", 3), ("near", 5), ("g2", 1), ("c", 0), ("g2", 3), ("g3", 1), ("g1", 4), ("near", 7),
    ("r1", 0), ("g3", 2), ("g3", 3), ("c", 1), ("g1", 6), ("c", 2), ("g2", 4), ("r2", 0),
    ("r1", 1), ("c", 3), ("g2", 6), ("r1", 2), ("g3", 5), ("g3", 4), ("r1", 3), ("r3", 0),
    ("r2", 1), ("g3", 6), ("c", 4), ("r2", 2), ("r2", 3), ("g3", 7), ("c", 5), ("r1", 4),
    ("c", 6), ("c", 7), ("r2", 4), ("r1", 5), ("r3", 1), ("r1", 6), ("r3", 2), ("r3", 3),
    ("r1", 7), ("r2", 5), ("r2", 6), ("r3", 4), ("r2", 7), ("wd", 0), ("r3", 5), ("r3", 6),
    ("r3", 7), ("wu", 0),
)


def gelu_parts(pre):
    phi = 0.5 * (1.0 + lax.erf(pre * math.sqrt(0.5)))
    act = pre * phi
    slope = phi + pre * jnp.exp(-0.5 * pre * pre) * (1.0 / math.sqrt(2.0 * math.pi))
    return act, slope


def nn(a, b):
    return jnp.dot(a, b, preferred_element_type=F32)


def nt(a, b):
    return lax.dot_general(a, b, (((1,), (1,)), ((), ())), preferred_element_type=F32)


def tn(a, b):
    return lax.dot_general(a, b, (((0,), (0,)), ((), ())), preferred_element_type=F32)


def kernel(
    tok_ref, cot_ref, gates_ref, ids_ref, wup_hbm, wdn_hbm,
    gt_out, gg_out, gup, gdn,
    wup, wdn, wup_t, wdn_t, pt0, pt1, raw, send, near, rows, gate_lines, gate_in, score_lines, score_in, scaled, delta,
    sib_send, sib_recv, own, m1s, m1r, m2s, m2r, sc_send, sc_recv, ret_send, ret_recv,
    w_sem,
    t_send, t_recv, n_send, n_recv, d_send, d_recv, gl_send, gl_recv, sl_send, sl_recv, ga_send, ga_recv, gb_send, gb_recv, a2_send, a2_recv, b2_send, b2_recv,
    gs_send, gs_recv, sib_ss, sib_rs, m1_ss, m1_rs, m2_ss, m2_rs, sc_ss, sc_rs, r_ss, r_rs,
):
    e, h = lax.axis_index("exp"), lax.axis_index("head")
    z, y = e // NY, lax.rem(e, NY)
    x, c = h // 2, lax.rem(h, 2)

    def head_of(xx, cc):
        return lax.rem(xx + NX, NX) * 2 + cc

    xr, xl, xo = lax.rem(x + 1, NX), lax.rem(x + NX - 1, NX), lax.rem(x + 2, NX)
    right, left = head_of(x + 1, c), head_of(x - 1, c)
    sib = x * 2 + (1 - c)

    def exp_of(zz, yy):
        return lax.rem(zz + NZ, NZ) * NY + lax.rem(yy + NY, NY)

    barrier = pltpu.get_barrier_semaphore()

    def greet_exp(i, carry):
        pl.semaphore_signal(barrier, inc=1, device_id=(lax.rem(e + i, EXP), h), device_id_type=MESH)
        return carry

    def greet_head(i, carry):
        pl.semaphore_signal(barrier, inc=1, device_id=(e, lax.rem(h + i, HEAD)), device_id_type=MESH)
        return carry

    lax.fori_loop(1, EXP, greet_exp, 0)
    lax.fori_loop(1, HEAD, greet_head, 0)

    load_up = pltpu.make_async_copy(wup_hbm.at[0], wup, w_sem.at[0])
    load_dn = pltpu.make_async_copy(wdn_hbm.at[0], wdn, w_sem.at[1])
    load_up.start()
    load_dn.start()

    lane = lax.broadcasted_iota(I32, (TOK, 128), 1)
    sub = lax.broadcasted_iota(I32, (TOK, 128), 0)

    def column(ref, k):
        line = ref[k:k + 1, :].astype(F32)
        return jnp.sum(jnp.where(lane == sub, line, 0.0), axis=1, keepdims=True)

    def offset_of(expert):
        return ((z - (expert >> 2)) & (NZ - 1)) * NY + ((y - (expert & (NY - 1))) & (NY - 1))

    r0, r1 = offset_of(column(ids_ref, 0).astype(I32)), offset_of(column(ids_ref, 1).astype(I32))
    first = jnp.zeros((1, 128), F32)
    for p, (dz, dy) in enumerate(ORDER):
        first = jnp.where(lane[0:1] == dz * NY + dy, float(p * CAP), first)
    oh0, oh1 = r0 == lane, r1 == lane
    both = (oh0 | oh1).astype(BF16)
    place = nn((lane < sub).astype(BF16), both) + first
    d0 = jnp.sum(jnp.where(oh0, place, 0.0), axis=1, keepdims=True).astype(I32)
    d1 = jnp.sum(jnp.where(oh1, place, 0.0), axis=1, keepdims=True).astype(I32)
    slots = lax.broadcasted_iota(I32, (TOK, ROWS), 1)
    pt0[...] = (d0 == slots).astype(BF16)
    pt1[...] = (d1 == slots).astype(BF16)
    gates = [jnp.broadcast_to(gates_ref[k:k + 1, :], (16, TOK)) for k in range(2)]
    gate_row = (nn(gates[0], pt0[...]) + nn(gates[1], pt1[...]))[0:1, :]
    for i in range(ROWS // LINE):
        gate_lines[i] = gate_row[:, i * LINE:(i + 1) * LINE]
    gate_in[HOME * PER] = gate_lines[HOME * PER // 8]
    slot_of = lax.broadcasted_iota(I32, (1, LINE), 1) // CAP

    def merge(ref, first, count):
        line = jnp.zeros((1, LINE), F32)
        for p in range(first, first + count):
            line = jnp.where(slot_of == p % 8, ref[p], line)
        return line

    def rows_of(k):
        return pl.ds(k * CH, CH)

    def sources(first, count=1):
        return range(first * PER + (first == HOME), (first + count) * PER)

    def others(first, count=1):
        skip = CAP if first == HOME else 0
        return pl.ds(first * CH + skip, count * CH - skip)

    def block(p):
        return pl.ds(p * CAP, CAP)

    def fill(k):
        here = rows_of(k)
        p0, p1 = pt0[:, here], pt1[:, here]
        send[here, :] = tn(p0 + p1, raw[x]).astype(BF16)

    def fill_near(k):
        here, there = rows_of(k), rows_of(NEAR.index(k))
        p0, p1 = pt0[:, here], pt1[:, here]
        for xx in range(NX):
            near[xx, there, :] = tn(p0 + p1, raw[xx]).astype(BF16)

    def remote(src, dst, ss, rs, exp_i, head_i):
        return pltpu.make_async_remote_copy(
            src_ref=src, dst_ref=dst, send_sem=ss, recv_sem=rs,
            device_id=(exp_i, head_i), device_id_type=MESH,
        )

    def send_gates(k):
        for p in sources(k):
            dz, dy = ORDER[p]
            remote(
                gate_lines.at[p // 8], gate_in.at[p], gl_send.at[0], gl_recv.at[k], exp_of(z - dz, y - dy), h
            ).start()

    def dispatch(k):
        for p in range(k * PER, (k + 1) * PER):
            dz, dy = ORDER[p]
            remote(
                send.at[block(p)], rows.at[c, x, block(p)], d_send.at[0], d_recv.at[k],
                exp_of(z - dz, y - dy), h,
            ).start()

    def dispatch_near(k):
        for p in sources(k):
            dz, dy = ORDER[p]
            remote(
                near.at[:, block(p + (NEAR.index(k) - k) * PER)], rows.at[c, :, block(p)],
                n_send.at[0], n_recv.at[k], exp_of(z - dz, y - dy), h,
            ).start()

    def wait_recv(ref, rs):
        remote(ref, ref, rs, rs, e, sib).wait_recv()

    def wait_send(ref, ss):
        remote(ref, ref, ss, ss, e, sib).wait_send()

    raw[x, :, 0:FL] = tok_ref[...]
    raw[x, :, FL:XD] = cot_ref[...]
    fill(FAR[0])
    pl.semaphore_wait(barrier, EXP - 1 + HEAD - 1)
    mine = raw.at[x]
    remote(mine, mine, t_send.at[0], t_recv.at[0], e, right).start()
    remote(mine, mine, t_send.at[1], t_recv.at[1], e, left).start()
    dispatch(FAR[0])
    for k in FAR[1:AHEAD]:
        fill(k)
        dispatch(k)
    for k in FAR[AHEAD:]:
        fill(k)
    for k in range(NCH):
        send_gates(k)
    load_up.wait()
    load_dn.wait()
    for hh in range(HEAD):
        part_of = pl.ds(hh * FL, FL)
        wup_t[:, part_of] = wup[part_of, :].T
        wdn_t[part_of, :] = wdn[:, part_of].T

    def pass_raw(k):
        low, high = raw.at[xl, pl.ds(0, TOK // 2)], raw.at[xr, pl.ds(TOK // 2, TOK // 2)]
        wait_recv(raw.at[xl], t_recv.at[0])
        remote(low, low, t_send.at[2], t_recv.at[2], e, right).start()
        wait_recv(raw.at[xr], t_recv.at[1])
        remote(high, high, t_send.at[3], t_recv.at[3], e, left).start()

    def send_near(k):
        if k == NEAR[0]:
            wait_recv(raw.at[xo, pl.ds(0, TOK // 2)], t_recv.at[2])
            wait_recv(raw.at[xo, pl.ds(TOK // 2, TOK // 2)], t_recv.at[3])
        fill_near(k)
        dispatch_near(k)
        if k == HOME:
            rows[c, :, HOME * CH:HOME * CH + CAP, :] = near[:, 0:CAP, :]

    def part(xx, k, start=0, size=CH):
        return rows.at[c, xx, pl.ds(k * CH + start, size)]

    def whole(cc, k):
        return rows.at[cc, :, rows_of(k)]

    half = CH // 2

    def gather1(k):
        if k in FAR:
            wait_recv(rows.at[c, x, rows_of(k)], d_recv.at[k])
            mine = part(x, k)
            remote(mine, mine, ga_send.at[0], ga_recv.at[k], e, right).start()
            remote(mine, mine, gb_send.at[0], gb_recv.at[k], e, left).start()
            remote(mine, mine, gs_send.at[0], gs_recv.at[k, 0], e, sib).start()

    def gather2(k):
        if k in FAR:
            low, high = part(xl, k, 0, half), part(xr, k, half, half)
            wait_recv(part(xl, k), ga_recv.at[k])
            remote(low, low, a2_send.at[0], a2_recv.at[k], e, right).start()
            remote(part(xl, k), part(xl, k), gs_send.at[1], gs_recv.at[k, 1], e, sib).start()
            wait_recv(part(xr, k), gb_recv.at[k])
            remote(high, high, b2_send.at[0], b2_recv.at[k], e, left).start()
            remote(part(xr, k), part(xr, k), gs_send.at[2], gs_recv.at[k, 2], e, sib).start()

    def gather3(k):
        if k in FAR:
            wait_recv(part(xo, k, 0, half), a2_recv.at[k])
            wait_recv(part(xo, k, half, half), b2_recv.at[k])
            remote(part(xo, k), part(xo, k), gs_send.at[3], gs_recv.at[k, 3], e, sib).start()
        else:
            wait_recv(rows.at[c, :, others(k)], n_recv.at[k])
            remote(whole(c, k), whole(c, k), gs_send.at[4], gs_recv.at[k, 0], e, sib).start()

    def gather4(k):
        if k in FAR:
            for i in range(4):
                wait_recv(part(x, k), gs_recv.at[k, i])
        else:
            wait_recv(whole(1 - c, k), gs_recv.at[k, 0])

    def eye(first, count):
        return lane[0:count * CH] == sub[0:count * CH] + first % 2 * CH

    def features(hh):
        return pl.ds(pl.multiple_of(hh * FL, FL), FL)

    def group_rows(g):
        first, count = GROUPS[g]
        return pl.ds(first * CH, count * CH)

    def compute(g):
        first, count = GROUPS[g]
        for k in range(first, first + count):
            gather4(k)
        here, high = group_rows(g), count * CH
        pre = jnp.zeros((high, HID), F32)
        back = jnp.zeros((high, HID), F32)
        for hh in range(HEAD):
            part_of = pl.ds(hh * FL, FL)
            pre = pre + nn(rows[hh % 2, hh // 2, here, 0:FL], wup[part_of, :])
            back = back + nn(rows[hh % 2, hh // 2, here, FL:XD], wdn_t[part_of, :])
        for k in range(first, first + count):
            places = sources(k)
            wait_recv(gate_in.at[pl.ds(places[0], len(places))], gl_recv.at[k])
        diagonal = eye(first, count)
        gate = merge(gate_in, first * PER, count * PER)
        g_column = jnp.sum(jnp.where(diagonal, gate, 0.0), axis=1, keepdims=True)
        act, slope = gelu_parts(pre)
        score = jnp.sum(back * act, axis=1, keepdims=True)
        scaled[here, :] = (g_column * act).astype(BF16)
        delta[here, :] = (g_column * back * slope).astype(BF16)
        terms = delta[here, :]
        for xx in range(NX):
            sib_send[xx, here, :] = nn(terms, wup_t[:, features(xx * 2 + (1 - c))]).astype(BF16)
        remote(sib_send.at[:, here], sib_recv.at[:, here], sib_ss.at[g], sib_rs.at[g], e, sib).start()
        line = jnp.sum(jnp.where(diagonal, score, 0.0), axis=0, keepdims=True)
        sc_send[g] = line
        sc_recv[g, h] = line

        def tell(i, carry):
            remote(
                sc_send.at[g], sc_recv.at[g, h], sc_ss.at[g], sc_rs.at[g], e, lax.rem(h + i, HEAD)
            ).start()
            return carry

        lax.fori_loop(1, HEAD, tell, 0)
        for xx in range(NX):
            own[xx, here, :] = nn(terms, wup_t[:, features(xx * 2 + c)])

    def pair(g, xx, start, size):
        here, cols = group_rows(g), pl.ds(start, size)
        return own[xx, here, cols] + sib_recv[xx, here, cols].astype(F32)

    hf = FL // 2

    def reduce1(g):
        here = group_rows(g)
        wait_recv(sib_recv.at[:, here], sib_rs.at[g])
        for i, to in enumerate((right, left)):
            m1s[i, here, :] = pair(g, xo, i * hf, hf).astype(BF16)
            remote(m1s.at[i, here], m1r.at[i, here], m1_ss.at[g, i], m1_rs.at[g, i], e, to).start()

    def reduce2(g):
        here = group_rows(g)
        m2s[0, here, hf:FL] = pair(g, xr, hf, hf).astype(BF16)
        m2s[1, here, 0:hf] = pair(g, xl, 0, hf).astype(BF16)
        for i, (at, to) in enumerate(((xr, right), (xl, left))):
            wait_recv(m1r.at[i, here], m1_rs.at[g, i])
            both = pair(g, at, i * hf, hf) + m1r[i, here, :].astype(F32)
            m2s[i, here, i * hf:(i + 1) * hf] = both.astype(BF16)
            remote(m2s.at[i, here], m2r.at[i, here], m2_ss.at[g, i], m2_rs.at[g, i], e, to).start()

    def reduce3(g):
        here, (first, count) = group_rows(g), GROUPS[g]
        wait_recv(sc_recv.at[g, pl.ds(0, HEAD - 1)], sc_rs.at[g])
        total = sc_recv[g, 0]
        for i in range(1, HEAD):
            total = total + sc_recv[g, i]
        score_lines[g] = total.astype(BF16).astype(F32)
        wait_recv(m2r.at[0, here], m2_rs.at[g, 0])
        wait_recv(m2r.at[1, here], m2_rs.at[g, 1])
        done = pair(g, x, 0, FL) + m2r[0, here, :].astype(F32) + m2r[1, here, :].astype(F32)
        ret_send[here, :] = done.astype(BF16)
        for p in sources(first, count):
            dz, dy = ORDER[p]
            to = exp_of(z + dz, y + dy)
            remote(
                ret_send.at[block(p)], ret_recv.at[block(p)], r_ss.at[0], r_rs.at[g], to, h
            ).start()
            remote(
                score_lines.at[g], score_in.at[p], sl_send.at[0], sl_recv.at[0], to, h
            ).start()
        if first == HOME:
            own_rows = pl.ds(HOME * CH, CAP)
            ret_recv[own_rows, :] = ret_send[own_rows, :]
            score_in[HOME * PER] = score_lines[g]

    def weights_down(k):
        flat = scaled[...].T
        for hh in range(HEAD):
            gdn[0, :, hh * FL:(hh + 1) * FL] = nn(flat, rows[hh % 2, hh // 2, :, FL:XD]).astype(BF16)

    def weights_up(k):
        for hh in range(HEAD):
            gup[0, hh * FL:(hh + 1) * FL, :] = tn(rows[hh % 2, hh // 2, :, 0:FL], delta[...]).astype(BF16)

    stages = {
        "pass": pass_raw, "d": dispatch, "near": send_near, "g1": gather1, "g2": gather2, "g3": gather3,
        "c": compute, "r1": reduce1, "r2": reduce2, "r3": reduce3, "wd": weights_down, "wu": weights_up,
    }
    for stage, k in PLAN:
        stages[stage](k)

    total = jnp.zeros((TOK, FL), F32)
    for g, (first, count) in enumerate(GROUPS):
        here = group_rows(g)
        wait_recv(ret_recv.at[others(first, count)], r_rs.at[g])
        total = total + nn(pt0[:, here] + pt1[:, here], ret_recv[here, :])
    gt_out[...] = total.astype(BF16)
    wait_recv(score_in.at[pl.ds(1, EXP - 1)], sl_recv.at[0])
    for k, pt in enumerate((pt0, pt1)):
        picked = jnp.zeros((TOK, LINE), F32)
        for i in range(ROWS // LINE):
            picked = picked + pt[:, i * LINE:(i + 1) * LINE].astype(F32) * merge(score_in, i * 8, 8)
        score = jnp.sum(picked, axis=1, keepdims=True)
        gg_out[k:k + 1, :] = jnp.sum(jnp.where(lane == sub, score, 0.0), axis=0, keepdims=True).astype(BF16)

    wait_send(raw.at[0], t_send.at[0])
    wait_send(raw.at[0], t_send.at[1])
    wait_send(raw.at[0, pl.ds(0, TOK // 2)], t_send.at[2])
    wait_send(raw.at[0, pl.ds(0, TOK // 2)], t_send.at[3])
    far_rows, near_rows = len(FAR) * CH, len(NEAR) * CH
    wait_send(send.at[pl.ds(0, far_rows)], d_send.at[0])
    wait_send(near.at[:, pl.ds(CAP, near_rows - CAP)], n_send.at[0])
    wait_send(gate_in.at[pl.ds(1, EXP - 1)], gl_send.at[0])
    wait_send(score_in.at[pl.ds(1, EXP - 1)], sl_send.at[0])
    gathered = rows.at[0, 0, pl.ds(0, far_rows)]
    wait_send(gathered, ga_send.at[0])
    wait_send(gathered, gb_send.at[0])
    for i in range(4):
        wait_send(gathered, gs_send.at[i])
    wait_send(rows.at[0, :, pl.ds(0, near_rows)], gs_send.at[4])
    halves = rows.at[0, 0, pl.ds(0, far_rows // 2)]
    wait_send(halves, a2_send.at[0])
    wait_send(halves, b2_send.at[0])
    for g in range(len(GROUPS)):
        here = group_rows(g)
        wait_send(sib_send.at[:, here], sib_ss.at[g])
        for i in range(2):
            wait_send(m1s.at[i, here], m1_ss.at[g, i])
            wait_send(m2s.at[i, here], m2_ss.at[g, i])
        wait_send(sc_recv.at[g, pl.ds(0, HEAD - 1)], sc_ss.at[g])
    wait_send(ret_send.at[pl.ds(CAP, ROWS - CAP)], r_ss.at[0])


def store(*refs):
    ins, outs, sem = refs[:4], refs[4:8], refs[8]
    copies = [pltpu.make_async_copy(ins[i], outs[i], sem.at[i]) for i in range(4)]
    for one in copies:
        one.start()
    for one in copies:
        one.wait()


def shards(tokens, cotangent, gates, expert_ids, w_up, w_down):
    vmem = pl.BlockSpec(memory_space=pltpu.VMEM)
    hbm = pl.BlockSpec(memory_space=pl.ANY)
    dma = pltpu.SemaphoreType.DMA
    shapes = ((TOK, FL), (2, TOK), (1, D, HID), (1, HID, D))
    results = pl.pallas_call(
        kernel,
        out_shape=tuple(pltpu.VMEM(shape, BF16) for shape in shapes),
        in_specs=[vmem, vmem, vmem, vmem, hbm, hbm],
        out_specs=(vmem, vmem, vmem, vmem),
        scratch_shapes=[
            pltpu.VMEM((D, HID), BF16),
            pltpu.VMEM((HID, D), BF16),
            pltpu.VMEM((HID, D), BF16),
            pltpu.VMEM((D, HID), BF16),
            pltpu.VMEM((TOK, ROWS), BF16),
            pltpu.VMEM((TOK, ROWS), BF16),
            pltpu.VMEM((NX, TOK, XD), BF16),
            pltpu.VMEM((ROWS, XD), BF16),
            pltpu.VMEM((NX, len(NEAR) * CH, XD), BF16),
            pltpu.VMEM((2, NX, ROWS, XD), BF16),
            pltpu.VMEM((ROWS // LINE, 1, LINE), F32),
            pltpu.VMEM((EXP, 1, LINE), F32),
            pltpu.VMEM((NCH, 1, LINE), F32),
            pltpu.VMEM((EXP, 1, LINE), F32),
            pltpu.VMEM((ROWS, HID), BF16),
            pltpu.VMEM((ROWS, HID), BF16),
            pltpu.VMEM((NX, ROWS, FL), BF16),
            pltpu.VMEM((NX, ROWS, FL), BF16),
            pltpu.VMEM((NX, ROWS, FL), F32),
            pltpu.VMEM((2, ROWS, FL // 2), BF16),
            pltpu.VMEM((2, ROWS, FL // 2), BF16),
            pltpu.VMEM((2, ROWS, FL), BF16),
            pltpu.VMEM((2, ROWS, FL), BF16),
            pltpu.VMEM((NCH, 1, LINE), F32),
            pltpu.VMEM((NCH, HEAD, 1, LINE), F32),
            pltpu.VMEM((ROWS, FL), BF16),
            pltpu.VMEM((ROWS, FL), BF16),
            dma((2,)),
            dma((4,)), dma((4,)),
            dma((1,)), dma((NCH,)),
            dma((1,)), dma((NCH,)),
            dma((1,)), dma((NCH,)),
            dma((1,)), dma((1,)),
            dma((1,)), dma((NCH,)),
            dma((1,)), dma((NCH,)),
            dma((1,)), dma((NCH,)),
            dma((1,)), dma((NCH,)),
            dma((5,)), dma((NCH, 4)),
            dma((NCH,)), dma((NCH,)),
            dma((NCH, 2)), dma((NCH, 2)),
            dma((NCH, 2)), dma((NCH, 2)),
            dma((NCH,)), dma((NCH,)),
            dma((1,)), dma((NCH,)),
        ],
        compiler_params=pltpu.CompilerParams(
            collective_id=0, has_side_effects=True, vmem_limit_bytes=56 * 1024 * 1024
        ),
        cost_estimate=pl.CostEstimate(
            flops=10 * ROWS * D * HID, bytes_accessed=8 * D * HID, transcendentals=2 * ROWS * HID
        ),
    )(tokens, cotangent, gates.T, expert_ids.T, w_up, w_down)
    grad_tokens, grad_gates, grad_up, grad_down = pl.pallas_call(
        store,
        out_shape=tuple(jax.ShapeDtypeStruct(shape, BF16) for shape in shapes),
        in_specs=[vmem] * 4,
        out_specs=(hbm,) * 4,
        scratch_shapes=[dma((4,))],
        compiler_params=pltpu.CompilerParams(vmem_limit_bytes=16 * 1024 * 1024),
    )(*results)
    return grad_tokens, grad_gates.T, grad_up, grad_down


def solution(mesh):
    return jax.shard_map(
        shards,
        mesh=mesh,
        in_specs=(
            P("exp", "head"),
            P("exp", "head"),
            P("exp", None),
            P("exp", None),
            P("exp", None, "head"),
            P("exp", "head", None),
        ),
        out_specs=(
            P("exp", "head"),
            P("exp", None),
            P("exp", None, "head"),
            P("exp", "head", None),
        ),
        check_vma=False,
    )
```

```python
import math

import jax
import jax.numpy as jnp
from jax import lax
from jax.experimental import pallas as pl
from jax.experimental.pallas import tpu as pltpu
from jax.sharding import PartitionSpec as P

MESH = pl.DeviceIdType.MESH
BF16, F32, I32 = jnp.bfloat16, jnp.float32, jnp.int32

NZ, NY, NX = 8, 4, 4
EXP, HEAD = NZ * NY, 2 * NX
CAP = 16
TOK = 128
PER = 4
CH = PER * CAP
NCH = EXP // PER
ROWS = NCH * CH
FL = 512
HID = 256
D = HEAD * FL
XD = 2 * FL
LINE = 128


def offsets():
    order = []
    for reach, late in ((2, 0), (3, 0), (0, 0), (3, 1), (4, 0), (1, 0), (2, 1), (1, 1)):
        if reach in (0, NZ // 2):
            order += [(reach, 0), (reach, 1), (reach, NY - 1), (reach, 2)]
        elif late:
            order += [(reach, NY - 1), (NZ - reach, 1), (reach, 2), (NZ - reach, 2)]
        else:
            order += [(reach, 0), (NZ - reach, 0), (reach, 1), (NZ - reach, NY - 1)]
    return order


ORDER = offsets()
HOME = 2
NEAR = (HOME, 5, 7)
FAR = (0, 1, 3, 4, 6)
AHEAD = 2
GROUPS = ((0, 1), (1, 1), (2, 1), (3, 1), (4, 1), (5, 1), (6, 1), (7, 1))
PLAN = (
    ("g1", 0), ("d", 3), ("pass", 0), ("g2", 0), ("g1", 1), ("d", 4), ("near", 2), ("g3", 0),
    ("g1", 3), ("d", 6), ("near", 5), ("g2", 1), ("c", 0), ("g2", 3), ("g3", 1), ("g1", 4),
    ("near", 7), ("r1", 0), ("g3", 2), ("g3", 3), ("c", 1), ("g1", 6), ("c", 2), ("g2", 4),
    ("r2", 0), ("r1", 1), ("c", 3), ("g2", 6), ("r1", 2), ("g3", 5), ("g3", 4), ("r1", 3),
    ("r3", 0), ("r2", 1), ("g3", 6), ("c", 4), ("r2", 2), ("r2", 3), ("g3", 7), ("c", 5),
    ("r1", 4), ("c", 6), ("c", 7), ("r2", 4), ("r1", 5), ("r3", 1), ("r1", 6), ("r3", 2),
    ("r3", 3), ("r1", 7), ("r2", 5), ("r2", 6), ("r3", 4), ("r2", 7), ("wd", 0), ("r3", 5),
    ("r3", 6), ("r3", 7), ("wu", 0),
)


def gelu_parts(pre):
    phi = 0.5 * (1.0 + lax.erf(pre * math.sqrt(0.5)))
    act = pre * phi
    slope = phi + pre * jnp.exp(-0.5 * pre * pre) * (1.0 / math.sqrt(2.0 * math.pi))
    return act, slope


def nn(a, b):
    return jnp.dot(a, b, preferred_element_type=F32)


def nt(a, b):
    return lax.dot_general(a, b, (((1,), (1,)), ((), ())), preferred_element_type=F32)


def tn(a, b):
    return lax.dot_general(a, b, (((0,), (0,)), ((), ())), preferred_element_type=F32)


def kernel(
    tok_ref, cot_ref, gates_ref, ids_ref, wup_hbm, wdn_hbm,
    gt_out, gg_out, gup, gdn,
    wup, wdn, wup_t, wdn_t, pt0, pt1, raw, send, near, rows, gate_lines, gate_in, score_lines, score_in, scaled, delta,
    sib_send, sib_recv, own, m1s, m1r, m2s, m2r, sc_send, sc_recv, ret_send, ret_recv,
    w_sem,
    t_send, t_recv, n_send, n_recv, d_send, d_recv, gl_send, gl_recv, sl_send, sl_recv, ga_send, ga_recv, gb_send, gb_recv, a2_send, a2_recv, b2_send, b2_recv,
    gs_send, gs_recv, sib_ss, sib_rs, m1_ss, m1_rs, m2_ss, m2_rs, sc_ss, sc_rs, r_ss, r_rs,
):
    e, h = lax.axis_index("exp"), lax.axis_index("head")
    z, y = e // NY, lax.rem(e, NY)
    x, c = h // 2, lax.rem(h, 2)

    def head_of(xx, cc):
        return lax.rem(xx + NX, NX) * 2 + cc

    xr, xl, xo = lax.rem(x + 1, NX), lax.rem(x + NX - 1, NX), lax.rem(x + 2, NX)
    right, left = head_of(x + 1, c), head_of(x - 1, c)
    sib = x * 2 + (1 - c)

    def exp_of(zz, yy):
        return lax.rem(zz + NZ, NZ) * NY + lax.rem(yy + NY, NY)

    barrier = pltpu.get_barrier_semaphore()

    def greet_exp(i, carry):
        pl.semaphore_signal(barrier, inc=1, device_id=(lax.rem(e + i, EXP), h), device_id_type=MESH)
        return carry

    def greet_head(i, carry):
        pl.semaphore_signal(barrier, inc=1, device_id=(e, lax.rem(h + i, HEAD)), device_id_type=MESH)
        return carry

    lax.fori_loop(1, EXP, greet_exp, 0)
    lax.fori_loop(1, HEAD, greet_head, 0)

    load_up = pltpu.make_async_copy(wup_hbm.at[0], wup, w_sem.at[0])
    load_dn = pltpu.make_async_copy(wdn_hbm.at[0], wdn, w_sem.at[1])
    load_up.start()
    load_dn.start()

    lane = lax.broadcasted_iota(I32, (TOK, 128), 1)
    sub = lax.broadcasted_iota(I32, (TOK, 128), 0)

    def column(ref, k):
        line = ref[k:k + 1, :].astype(F32)
        return jnp.sum(jnp.where(lane == sub, line, 0.0), axis=1, keepdims=True)

    def offset_of(expert):
        return ((z - (expert >> 2)) & (NZ - 1)) * NY + ((y - (expert & (NY - 1))) & (NY - 1))

    r0, r1 = offset_of(column(ids_ref, 0).astype(I32)), offset_of(column(ids_ref, 1).astype(I32))
    first = jnp.zeros((1, 128), F32)
    for p, (dz, dy) in enumerate(ORDER):
        first = jnp.where(lane[0:1] == dz * NY + dy, float(p * CAP), first)
    oh0, oh1 = r0 == lane, r1 == lane
    both = (oh0 | oh1).astype(BF16)
    place = nn((lane < sub).astype(BF16), both) + first
    d0 = jnp.sum(jnp.where(oh0, place, 0.0), axis=1, keepdims=True).astype(I32)
    d1 = jnp.sum(jnp.where(oh1, place, 0.0), axis=1, keepdims=True).astype(I32)
    slots = lax.broadcasted_iota(I32, (TOK, ROWS), 1)
    pt0[...] = (d0 == slots).astype(BF16)
    pt1[...] = (d1 == slots).astype(BF16)
    gates = [jnp.broadcast_to(gates_ref[k:k + 1, :], (16, TOK)) for k in range(2)]
    gate_row = (nn(gates[0], pt0[...]) + nn(gates[1], pt1[...]))[0:1, :]
    for i in range(ROWS // LINE):
        gate_lines[i] = gate_row[:, i * LINE:(i + 1) * LINE]
    gate_in[HOME * PER] = gate_lines[HOME * PER // 8]
    slot_of = lax.broadcasted_iota(I32, (1, LINE), 1) // CAP

    def merge(ref, first, count):
        line = jnp.zeros((1, LINE), F32)
        for p in range(first, first + count):
            line = jnp.where(slot_of == p % 8, ref[p], line)
        return line

    def rows_of(k):
        return pl.ds(k * CH, CH)

    def sources(first, count=1):
        return range(first * PER + (first == HOME), (first + count) * PER)

    def others(first, count=1):
        skip = CAP if first == HOME else 0
        return pl.ds(first * CH + skip, count * CH - skip)

    def block(p):
        return pl.ds(p * CAP, CAP)

    def fill(k):
        here = rows_of(k)
        p0, p1 = pt0[:, here], pt1[:, here]
        send[here, :] = tn(p0 + p1, raw[x]).astype(BF16)

    def fill_near(k):
        here, there = rows_of(k), rows_of(NEAR.index(k))
        p0, p1 = pt0[:, here], pt1[:, here]
        for xx in range(NX):
            near[xx, there, :] = tn(p0 + p1, raw[xx]).astype(BF16)

    def remote(src, dst, ss, rs, exp_i, head_i):
        return pltpu.make_async_remote_copy(
            src_ref=src, dst_ref=dst, send_sem=ss, recv_sem=rs,
            device_id=(exp_i, head_i), device_id_type=MESH,
        )

    def send_gates(k):
        for p in sources(k):
            dz, dy = ORDER[p]
            remote(
                gate_lines.at[p // 8], gate_in.at[p], gl_send.at[0], gl_recv.at[k], exp_of(z - dz, y - dy), h
            ).start()

    def dispatch(k):
        for p in range(k * PER, (k + 1) * PER):
            dz, dy = ORDER[p]
            remote(
                send.at[block(p)], rows.at[c, x, block(p)], d_send.at[0], d_recv.at[k],
                exp_of(z - dz, y - dy), h,
            ).start()

    def dispatch_near(k):
        for p in sources(k):
            dz, dy = ORDER[p]
            remote(
                near.at[:, block(p + (NEAR.index(k) - k) * PER)], rows.at[c, :, block(p)],
                n_send.at[0], n_recv.at[k], exp_of(z - dz, y - dy), h,
            ).start()

    def wait_recv(ref, rs):
        remote(ref, ref, rs, rs, e, sib).wait_recv()

    def wait_send(ref, ss):
        remote(ref, ref, ss, ss, e, sib).wait_send()

    raw[x, :, 0:FL] = tok_ref[...]
    raw[x, :, FL:XD] = cot_ref[...]
    fill(FAR[0])
    pl.semaphore_wait(barrier, EXP - 1 + HEAD - 1)
    mine = raw.at[x]
    remote(mine, mine, t_send.at[0], t_recv.at[0], e, right).start()
    remote(mine, mine, t_send.at[1], t_recv.at[1], e, left).start()
    dispatch(FAR[0])
    for k in FAR[1:AHEAD]:
        fill(k)
        dispatch(k)
    for k in FAR[AHEAD:]:
        fill(k)
    for k in range(NCH):
        send_gates(k)
    load_up.wait()
    load_dn.wait()
    for hh in range(HEAD):
        part_of = pl.ds(hh * FL, FL)
        wup_t[:, part_of] = wup[part_of, :].T
        wdn_t[part_of, :] = wdn[:, part_of].T

    def pass_raw(k):
        low, high = raw.at[xl, pl.ds(0, TOK // 2)], raw.at[xr, pl.ds(TOK // 2, TOK // 2)]
        wait_recv(raw.at[xl], t_recv.at[0])
        remote(low, low, t_send.at[2], t_recv.at[2], e, right).start()
        wait_recv(raw.at[xr], t_recv.at[1])
        remote(high, high, t_send.at[3], t_recv.at[3], e, left).start()

    def send_near(k):
        if k == NEAR[0]:
            wait_recv(raw.at[xo, pl.ds(0, TOK // 2)], t_recv.at[2])
            wait_recv(raw.at[xo, pl.ds(TOK // 2, TOK // 2)], t_recv.at[3])
        fill_near(k)
        dispatch_near(k)
        if k == HOME:
            rows[c, :, HOME * CH:HOME * CH + CAP, :] = near[:, 0:CAP, :]

    def part(xx, k, start=0, size=CH):
        return rows.at[c, xx, pl.ds(k * CH + start, size)]

    def whole(cc, k):
        return rows.at[cc, :, rows_of(k)]

    half = CH // 2

    def gather1(k):
        if k in FAR:
            wait_recv(rows.at[c, x, rows_of(k)], d_recv.at[k])
            mine = part(x, k)
            remote(mine, mine, ga_send.at[0], ga_recv.at[k], e, right).start()
            remote(mine, mine, gb_send.at[0], gb_recv.at[k], e, left).start()
            remote(mine, mine, gs_send.at[0], gs_recv.at[k, 0], e, sib).start()

    def gather2(k):
        if k in FAR:
            low, high = part(xl, k, 0, half), part(xr, k, half, half)
            wait_recv(part(xl, k), ga_recv.at[k])
            remote(low, low, a2_send.at[0], a2_recv.at[k], e, right).start()
            remote(part(xl, k), part(xl, k), gs_send.at[1], gs_recv.at[k, 1], e, sib).start()
            wait_recv(part(xr, k), gb_recv.at[k])
            remote(high, high, b2_send.at[0], b2_recv.at[k], e, left).start()
            remote(part(xr, k), part(xr, k), gs_send.at[2], gs_recv.at[k, 2], e, sib).start()

    def gather3(k):
        if k in FAR:
            wait_recv(part(xo, k, 0, half), a2_recv.at[k])
            wait_recv(part(xo, k, half, half), b2_recv.at[k])
            remote(part(xo, k), part(xo, k), gs_send.at[3], gs_recv.at[k, 3], e, sib).start()
        else:
            wait_recv(rows.at[c, :, others(k)], n_recv.at[k])
            remote(whole(c, k), whole(c, k), gs_send.at[4], gs_recv.at[k, 0], e, sib).start()

    def gather4(k):
        if k in FAR:
            for i in range(4):
                wait_recv(part(x, k), gs_recv.at[k, i])
        else:
            wait_recv(whole(1 - c, k), gs_recv.at[k, 0])

    def eye(first, count):
        return lane[0:count * CH] == sub[0:count * CH] + first % 2 * CH

    def features(hh):
        return pl.ds(pl.multiple_of(hh * FL, FL), FL)

    def group_rows(g):
        first, count = GROUPS[g]
        return pl.ds(first * CH, count * CH)

    def compute(g):
        first, count = GROUPS[g]
        for k in range(first, first + count):
            gather4(k)
        here, high = group_rows(g), count * CH
        pre = jnp.zeros((high, HID), F32)
        back = jnp.zeros((high, HID), F32)
        for hh in range(HEAD):
            part_of = pl.ds(hh * FL, FL)
            pre = pre + nn(rows[hh % 2, hh // 2, here, 0:FL], wup[part_of, :])
            back = back + nn(rows[hh % 2, hh // 2, here, FL:XD], wdn_t[part_of, :])
        for k in range(first, first + count):
            places = sources(k)
            wait_recv(gate_in.at[pl.ds(places[0], len(places))], gl_recv.at[k])
        diagonal = eye(first, count)
        gate = merge(gate_in, first * PER, count * PER)
        g_column = jnp.sum(jnp.where(diagonal, gate, 0.0), axis=1, keepdims=True)
        act, slope = gelu_parts(pre)
        score = jnp.sum(back * act, axis=1, keepdims=True)
        scaled[here, :] = (g_column * act).astype(BF16)
        delta[here, :] = (g_column * back * slope).astype(BF16)
        terms = delta[here, :]
        for xx in range(NX):
            sib_send[xx, here, :] = nn(terms, wup_t[:, features(xx * 2 + (1 - c))]).astype(BF16)
        remote(sib_send.at[:, here], sib_recv.at[:, here], sib_ss.at[g], sib_rs.at[g], e, sib).start()
        line = jnp.sum(jnp.where(diagonal, score, 0.0), axis=0, keepdims=True)
        sc_send[g] = line
        sc_recv[g, h] = line

        def tell(i, carry):
            remote(
                sc_send.at[g], sc_recv.at[g, h], sc_ss.at[g], sc_rs.at[g], e, lax.rem(h + i, HEAD)
            ).start()
            return carry

        lax.fori_loop(1, HEAD, tell, 0)
        for xx in range(NX):
            own[xx, here, :] = nn(terms, wup_t[:, features(xx * 2 + c)])

    def pair(g, xx, start, size):
        here, cols = group_rows(g), pl.ds(start, size)
        return own[xx, here, cols] + sib_recv[xx, here, cols].astype(F32)

    hf = FL // 2

    def reduce1(g):
        here = group_rows(g)
        wait_recv(sib_recv.at[:, here], sib_rs.at[g])
        for i, to in enumerate((right, left)):
            m1s[i, here, :] = pair(g, xo, i * hf, hf).astype(BF16)
            remote(m1s.at[i, here], m1r.at[i, here], m1_ss.at[g, i], m1_rs.at[g, i], e, to).start()

    def reduce2(g):
        here = group_rows(g)
        m2s[0, here, hf:FL] = pair(g, xr, hf, hf).astype(BF16)
        m2s[1, here, 0:hf] = pair(g, xl, 0, hf).astype(BF16)
        for i, (at, to) in enumerate(((xr, right), (xl, left))):
            wait_recv(m1r.at[i, here], m1_rs.at[g, i])
            both = pair(g, at, i * hf, hf) + m1r[i, here, :].astype(F32)
            m2s[i, here, i * hf:(i + 1) * hf] = both.astype(BF16)
            remote(m2s.at[i, here], m2r.at[i, here], m2_ss.at[g, i], m2_rs.at[g, i], e, to).start()

    def reduce3(g):
        here, (first, count) = group_rows(g), GROUPS[g]
        wait_recv(sc_recv.at[g, pl.ds(0, HEAD - 1)], sc_rs.at[g])
        total = sc_recv[g, 0]
        for i in range(1, HEAD):
            total = total + sc_recv[g, i]
        score_lines[g] = total.astype(BF16).astype(F32)
        wait_recv(m2r.at[0, here], m2_rs.at[g, 0])
        wait_recv(m2r.at[1, here], m2_rs.at[g, 1])
        done = pair(g, x, 0, FL) + m2r[0, here, :].astype(F32) + m2r[1, here, :].astype(F32)
        ret_send[here, :] = done.astype(BF16)
        for p in sources(first, count):
            dz, dy = ORDER[p]
            to = exp_of(z + dz, y + dy)
            remote(
                ret_send.at[block(p)], ret_recv.at[block(p)], r_ss.at[0], r_rs.at[g], to, h
            ).start()
            remote(
                score_lines.at[g], score_in.at[p], sl_send.at[0], sl_recv.at[0], to, h
            ).start()
        if first == HOME:
            own_rows = pl.ds(HOME * CH, CAP)
            ret_recv[own_rows, :] = ret_send[own_rows, :]
            score_in[HOME * PER] = score_lines[g]

    def weights_down(k):
        flat = scaled[...].T
        for hh in range(HEAD):
            gdn[0, :, hh * FL:(hh + 1) * FL] = nn(flat, rows[hh % 2, hh // 2, :, FL:XD]).astype(BF16)

    def weights_up(k):
        for hh in range(HEAD):
            gup[0, hh * FL:(hh + 1) * FL, :] = tn(rows[hh % 2, hh // 2, :, 0:FL], delta[...]).astype(BF16)

    stages = {
        "pass": pass_raw, "d": dispatch, "near": send_near, "g1": gather1, "g2": gather2, "g3": gather3,
        "c": compute, "r1": reduce1, "r2": reduce2, "r3": reduce3, "wd": weights_down, "wu": weights_up,
    }
    for stage, k in PLAN:
        stages[stage](k)

    total = jnp.zeros((TOK, FL), F32)
    for g, (first, count) in enumerate(GROUPS):
        here = group_rows(g)
        wait_recv(ret_recv.at[others(first, count)], r_rs.at[g])
        total = total + nn(pt0[:, here] + pt1[:, here], ret_recv[here, :])
    gt_out[...] = total.astype(BF16)
    wait_recv(score_in.at[pl.ds(1, EXP - 1)], sl_recv.at[0])
    for k, pt in enumerate((pt0, pt1)):
        picked = jnp.zeros((TOK, LINE), F32)
        for i in range(ROWS // LINE):
            picked = picked + pt[:, i * LINE:(i + 1) * LINE].astype(F32) * merge(score_in, i * 8, 8)
        score = jnp.sum(picked, axis=1, keepdims=True)
        gg_out[k:k + 1, :] = jnp.sum(jnp.where(lane == sub, score, 0.0), axis=0, keepdims=True).astype(BF16)

    wait_send(raw.at[0], t_send.at[0])
    wait_send(raw.at[0], t_send.at[1])
    wait_send(raw.at[0, pl.ds(0, TOK // 2)], t_send.at[2])
    wait_send(raw.at[0, pl.ds(0, TOK // 2)], t_send.at[3])
    far_rows, near_rows = len(FAR) * CH, len(NEAR) * CH
    wait_send(send.at[pl.ds(0, far_rows)], d_send.at[0])
    wait_send(near.at[:, pl.ds(CAP, near_rows - CAP)], n_send.at[0])
    wait_send(gate_in.at[pl.ds(1, EXP - 1)], gl_send.at[0])
    wait_send(score_in.at[pl.ds(1, EXP - 1)], sl_send.at[0])
    gathered = rows.at[0, 0, pl.ds(0, far_rows)]
    wait_send(gathered, ga_send.at[0])
    wait_send(gathered, gb_send.at[0])
    for i in range(4):
        wait_send(gathered, gs_send.at[i])
    wait_send(rows.at[0, :, pl.ds(0, near_rows)], gs_send.at[4])
    halves = rows.at[0, 0, pl.ds(0, far_rows // 2)]
    wait_send(halves, a2_send.at[0])
    wait_send(halves, b2_send.at[0])
    for g in range(len(GROUPS)):
        here = group_rows(g)
        wait_send(sib_send.at[:, here], sib_ss.at[g])
        for i in range(2):
            wait_send(m1s.at[i, here], m1_ss.at[g, i])
            wait_send(m2s.at[i, here], m2_ss.at[g, i])
        wait_send(sc_recv.at[g, pl.ds(0, HEAD - 1)], sc_ss.at[g])
    wait_send(ret_send.at[pl.ds(CAP, ROWS - CAP)], r_ss.at[0])


def store(*refs):
    ins, outs, sem = refs[:4], refs[4:8], refs[8]
    copies = [pltpu.make_async_copy(ins[i], outs[i], sem.at[i]) for i in range(4)]
    for one in copies:
        one.start()
    for one in copies:
        one.wait()


def shards(tokens, cotangent, gates, expert_ids, w_up, w_down):
    vmem = pl.BlockSpec(memory_space=pltpu.VMEM)
    hbm = pl.BlockSpec(memory_space=pl.ANY)
    dma = pltpu.SemaphoreType.DMA
    shapes = ((TOK, FL), (2, TOK), (1, D, HID), (1, HID, D))
    results = pl.pallas_call(
        kernel,
        out_shape=tuple(pltpu.VMEM(shape, BF16) for shape in shapes),
        in_specs=[vmem, vmem, vmem, vmem, hbm, hbm],
        out_specs=(vmem, vmem, vmem, vmem),
        scratch_shapes=[
            pltpu.VMEM((D, HID), BF16),
            pltpu.VMEM((HID, D), BF16),
            pltpu.VMEM((HID, D), BF16),
            pltpu.VMEM((D, HID), BF16),
            pltpu.VMEM((TOK, ROWS), BF16),
            pltpu.VMEM((TOK, ROWS), BF16),
            pltpu.VMEM((NX, TOK, XD), BF16),
            pltpu.VMEM((ROWS, XD), BF16),
            pltpu.VMEM((NX, len(NEAR) * CH, XD), BF16),
            pltpu.VMEM((2, NX, ROWS, XD), BF16),
            pltpu.VMEM((ROWS // LINE, 1, LINE), F32),
            pltpu.VMEM((EXP, 1, LINE), F32),
            pltpu.VMEM((NCH, 1, LINE), F32),
            pltpu.VMEM((EXP, 1, LINE), F32),
            pltpu.VMEM((ROWS, HID), BF16),
            pltpu.VMEM((ROWS, HID), BF16),
            pltpu.VMEM((NX, ROWS, FL), BF16),
            pltpu.VMEM((NX, ROWS, FL), BF16),
            pltpu.VMEM((NX, ROWS, FL), F32),
            pltpu.VMEM((2, ROWS, FL // 2), BF16),
            pltpu.VMEM((2, ROWS, FL // 2), BF16),
            pltpu.VMEM((2, ROWS, FL), BF16),
            pltpu.VMEM((2, ROWS, FL), BF16),
            pltpu.VMEM((NCH, 1, LINE), F32),
            pltpu.VMEM((NCH, HEAD, 1, LINE), F32),
            pltpu.VMEM((ROWS, FL), BF16),
            pltpu.VMEM((ROWS, FL), BF16),
            dma((2,)),
            dma((4,)), dma((4,)),
            dma((1,)), dma((NCH,)),
            dma((1,)), dma((NCH,)),
            dma((1,)), dma((NCH,)),
            dma((1,)), dma((1,)),
            dma((1,)), dma((NCH,)),
            dma((1,)), dma((NCH,)),
            dma((1,)), dma((NCH,)),
            dma((1,)), dma((NCH,)),
            dma((5,)), dma((NCH, 4)),
            dma((NCH,)), dma((NCH,)),
            dma((NCH, 2)), dma((NCH, 2)),
            dma((NCH, 2)), dma((NCH, 2)),
            dma((NCH,)), dma((NCH,)),
            dma((1,)), dma((NCH,)),
        ],
        compiler_params=pltpu.CompilerParams(
            collective_id=0, has_side_effects=True, vmem_limit_bytes=56 * 1024 * 1024
        ),
        cost_estimate=pl.CostEstimate(
            flops=10 * ROWS * D * HID, bytes_accessed=8 * D * HID, transcendentals=2 * ROWS * HID
        ),
    )(tokens, cotangent, gates.T, expert_ids.T, w_up, w_down)
    grad_tokens, grad_gates, grad_up, grad_down = pl.pallas_call(
        store,
        out_shape=tuple(jax.ShapeDtypeStruct(shape, BF16) for shape in shapes),
        in_specs=[vmem] * 4,
        out_specs=(hbm,) * 4,
        scratch_shapes=[dma((4,))],
        compiler_params=pltpu.CompilerParams(vmem_limit_bytes=16 * 1024 * 1024),
    )(*results)
    return grad_tokens, grad_gates.T, grad_up, grad_down


def solution(mesh):
    return jax.shard_map(
        shards,
        mesh=mesh,
        in_specs=(
            P("exp", "head"),
            P("exp", "head"),
            P("exp", None),
            P("exp", None),
            P("exp", None, "head"),
            P("exp", "head", None),
        ),
        out_specs=(
            P("exp", "head"),
            P("exp", None),
            P("exp", None, "head"),
            P("exp", "head", None),
        ),
        check_vma=False,
    )
```

```python
import math

import jax
import jax.numpy as jnp
from jax import lax
from jax.experimental import pallas as pl
from jax.experimental.pallas import tpu as pltpu
from jax.sharding import PartitionSpec as P

MESH = pl.DeviceIdType.MESH
BF16, F32, I32 = jnp.bfloat16, jnp.float32, jnp.int32

NZ, NY, NX = 8, 4, 4
EXP, HEAD = NZ * NY, 2 * NX
CAP = 16
TOK = 128
PER = 4
CH = PER * CAP
NCH = EXP // PER
ROWS = NCH * CH
FL = 512
HID = 256
D = HEAD * FL
XD = 2 * FL
LINE = 128


def offsets():
    order = []
    for reach, late in ((2, 0), (3, 0), (0, 0), (3, 1), (4, 0), (1, 0), (2, 1), (1, 1)):
        if reach in (0, NZ // 2):
            order += [(reach, 0), (reach, 1), (reach, NY - 1), (reach, 2)]
        elif late:
            order += [(reach, NY - 1), (NZ - reach, 1), (reach, 2), (NZ - reach, 2)]
        else:
            order += [(reach, 0), (NZ - reach, 0), (reach, 1), (NZ - reach, NY - 1)]
    return order


ORDER = offsets()
HOME = 2
NEAR = (HOME, 5, 7)
FAR = (0, 1, 3, 4, 6)
AHEAD = 2
GROUPS = ((0, 1), (1, 1), (2, 1), (3, 1), (4, 1), (5, 1), (6, 1), (7, 1))
PLAN = (
    ("g1", 0), ("d", 3), ("pass", 0), ("g2", 0), ("g1", 1), ("d", 4), ("near", 2), ("g3", 0),
    ("g1", 3), ("d", 6), ("near", 5), ("g2", 1), ("c", 0), ("g2", 3), ("g3", 1), ("g1", 4),
    ("near", 7), ("r1", 0), ("g3", 2), ("g3", 3), ("c", 1), ("g1", 6), ("c", 2), ("g2", 4),
    ("r2", 0), ("r1", 1), ("c", 3), ("g2", 6), ("r1", 2), ("g3", 5), ("g3", 4), ("r1", 3),
    ("r3", 0), ("r2", 1), ("g3", 6), ("c", 4), ("r2", 2), ("r2", 3), ("g3", 7), ("c", 5),
    ("r1", 4), ("c", 6), ("c", 7), ("r2", 4), ("r1", 5), ("r3", 1), ("r1", 6), ("r3", 2),
    ("r3", 3), ("r1", 7), ("r2", 5), ("r2", 6), ("r3", 4), ("r2", 7), ("wd", 0), ("r3", 5),
    ("r3", 6), ("r3", 7), ("wu", 0),
)


def gelu_parts(pre):
    phi = 0.5 * (1.0 + lax.erf(pre * math.sqrt(0.5)))
    act = pre * phi
    slope = phi + pre * jnp.exp(-0.5 * pre * pre) * (1.0 / math.sqrt(2.0 * math.pi))
    return act, slope


def nn(a, b):
    return jnp.dot(a, b, preferred_element_type=F32)


def nt(a, b):
    return lax.dot_general(a, b, (((1,), (1,)), ((), ())), preferred_element_type=F32)


def tn(a, b):
    return lax.dot_general(a, b, (((0,), (0,)), ((), ())), preferred_element_type=F32)


def kernel(
    tok_ref, cot_ref, gates_ref, ids_ref, wup_hbm, wdn_hbm,
    gt_out, gg_out, gup, gdn,
    wup, wdn, wup_t, wdn_t, pt0, pt1, raw, send, near, rows, gate_lines, gate_in, score_lines, score_in, scaled, delta,
    sib_send, sib_recv, own, m1s, m1r, m2s, m2r, sc_send, sc_recv, ret_send, ret_recv,
    w_sem,
    t_send, t_recv, n_send, n_recv, d_send, d_recv, gl_send, gl_recv, sl_send, sl_recv, ga_send, ga_recv, gb_send, gb_recv, a2_send, a2_recv, b2_send, b2_recv,
    gs_send, gs_recv, sib_ss, sib_rs, m1_ss, m1_rs, m2_ss, m2_rs, sc_ss, sc_rs, r_ss, r_rs,
):
    e, h = lax.axis_index("exp"), lax.axis_index("head")
    z, y = e // NY, lax.rem(e, NY)
    x, c = h // 2, lax.rem(h, 2)

    def head_of(xx, cc):
        return lax.rem(xx + NX, NX) * 2 + cc

    xr, xl, xo = lax.rem(x + 1, NX), lax.rem(x + NX - 1, NX), lax.rem(x + 2, NX)
    right, left = head_of(x + 1, c), head_of(x - 1, c)
    sib = x * 2 + (1 - c)

    def exp_of(zz, yy):
        return lax.rem(zz + NZ, NZ) * NY + lax.rem(yy + NY, NY)

    barrier = pltpu.get_barrier_semaphore()

    def greet_exp(i, carry):
        pl.semaphore_signal(barrier, inc=1, device_id=(lax.rem(e + i, EXP), h), device_id_type=MESH)
        return carry

    def greet_head(i, carry):
        pl.semaphore_signal(barrier, inc=1, device_id=(e, lax.rem(h + i, HEAD)), device_id_type=MESH)
        return carry

    lax.fori_loop(1, EXP, greet_exp, 0)
    lax.fori_loop(1, HEAD, greet_head, 0)

    load_up = pltpu.make_async_copy(wup_hbm.at[0], wup, w_sem.at[0])
    load_dn = pltpu.make_async_copy(wdn_hbm.at[0], wdn, w_sem.at[1])
    load_up.start()
    load_dn.start()

    lane = lax.broadcasted_iota(I32, (TOK, 128), 1)
    sub = lax.broadcasted_iota(I32, (TOK, 128), 0)

    def column(ref, k):
        line = ref[k:k + 1, :].astype(F32)
        return jnp.sum(jnp.where(lane == sub, line, 0.0), axis=1, keepdims=True)

    def offset_of(expert):
        return ((z - (expert >> 2)) & (NZ - 1)) * NY + ((y - (expert & (NY - 1))) & (NY - 1))

    r0, r1 = offset_of(column(ids_ref, 0).astype(I32)), offset_of(column(ids_ref, 1).astype(I32))
    first = jnp.zeros((1, 128), F32)
    for p, (dz, dy) in enumerate(ORDER):
        first = jnp.where(lane[0:1] == dz * NY + dy, float(p * CAP), first)
    oh0, oh1 = r0 == lane, r1 == lane
    both = (oh0 | oh1).astype(BF16)
    place = nn((lane < sub).astype(BF16), both) + first
    d0 = jnp.sum(jnp.where(oh0, place, 0.0), axis=1, keepdims=True).astype(I32)
    d1 = jnp.sum(jnp.where(oh1, place, 0.0), axis=1, keepdims=True).astype(I32)
    slots = lax.broadcasted_iota(I32, (TOK, ROWS), 1)
    pt0[...] = (d0 == slots).astype(BF16)
    pt1[...] = (d1 == slots).astype(BF16)
    gates = [jnp.broadcast_to(gates_ref[k:k + 1, :], (16, TOK)) for k in range(2)]
    gate_row = (nn(gates[0], pt0[...]) + nn(gates[1], pt1[...]))[0:1, :]
    for i in range(ROWS // LINE):
        gate_lines[i] = gate_row[:, i * LINE:(i + 1) * LINE]
    gate_in[HOME * PER] = gate_lines[HOME * PER // 8]
    slot_of = lax.broadcasted_iota(I32, (1, LINE), 1) // CAP

    def merge(ref, first, count):
        line = jnp.zeros((1, LINE), F32)
        for p in range(first, first + count):
            line = jnp.where(slot_of == p % 8, ref[p], line)
        return line

    def rows_of(k):
        return pl.ds(k * CH, CH)

    def sources(first, count=1):
        return range(first * PER + (first == HOME), (first + count) * PER)

    def others(first, count=1):
        skip = CAP if first == HOME else 0
        return pl.ds(first * CH + skip, count * CH - skip)

    def block(p):
        return pl.ds(p * CAP, CAP)

    def fill(k):
        here = rows_of(k)
        p0, p1 = pt0[:, here], pt1[:, here]
        send[here, :] = tn(p0 + p1, raw[x]).astype(BF16)

    def fill_near(k):
        here, there = rows_of(k), rows_of(NEAR.index(k))
        p0, p1 = pt0[:, here], pt1[:, here]
        for xx in range(NX):
            near[xx, there, :] = tn(p0 + p1, raw[xx]).astype(BF16)

    def remote(src, dst, ss, rs, exp_i, head_i):
        return pltpu.make_async_remote_copy(
            src_ref=src, dst_ref=dst, send_sem=ss, recv_sem=rs,
            device_id=(exp_i, head_i), device_id_type=MESH,
        )

    def send_gates(k):
        for p in sources(k):
            dz, dy = ORDER[p]
            remote(
                gate_lines.at[p // 8], gate_in.at[p], gl_send.at[0], gl_recv.at[k], exp_of(z - dz, y - dy), h
            ).start()

    def dispatch(k):
        for p in range(k * PER, (k + 1) * PER):
            dz, dy = ORDER[p]
            remote(
                send.at[block(p)], rows.at[c, x, block(p)], d_send.at[0], d_recv.at[k],
                exp_of(z - dz, y - dy), h,
            ).start()

    def dispatch_near(k):
        for p in sources(k):
            dz, dy = ORDER[p]
            remote(
                near.at[:, block(p + (NEAR.index(k) - k) * PER)], rows.at[c, :, block(p)],
                n_send.at[0], n_recv.at[k], exp_of(z - dz, y - dy), h,
            ).start()

    def wait_recv(ref, rs):
        remote(ref, ref, rs, rs, e, sib).wait_recv()

    def wait_send(ref, ss):
        remote(ref, ref, ss, ss, e, sib).wait_send()

    raw[x, :, 0:FL] = tok_ref[...]
    raw[x, :, FL:XD] = cot_ref[...]
    fill(FAR[0])
    pl.semaphore_wait(barrier, EXP - 1 + HEAD - 1)
    mine = raw.at[x]
    remote(mine, mine, t_send.at[0], t_recv.at[0], e, right).start()
    remote(mine, mine, t_send.at[1], t_recv.at[1], e, left).start()
    dispatch(FAR[0])
    for k in FAR[1:AHEAD]:
        fill(k)
        dispatch(k)
    for k in FAR[AHEAD:]:
        fill(k)
    for k in range(NCH):
        send_gates(k)
    load_up.wait()
    load_dn.wait()
    for hh in range(HEAD):
        part_of = pl.ds(hh * FL, FL)
        wup_t[:, part_of] = wup[part_of, :].T
        wdn_t[part_of, :] = wdn[:, part_of].T

    def pass_raw(k):
        low, high = raw.at[xl, pl.ds(0, TOK // 2)], raw.at[xr, pl.ds(TOK // 2, TOK // 2)]
        wait_recv(raw.at[xl], t_recv.at[0])
        remote(low, low, t_send.at[2], t_recv.at[2], e, right).start()
        wait_recv(raw.at[xr], t_recv.at[1])
        remote(high, high, t_send.at[3], t_recv.at[3], e, left).start()

    def send_near(k):
        if k == NEAR[0]:
            wait_recv(raw.at[xo, pl.ds(0, TOK // 2)], t_recv.at[2])
            wait_recv(raw.at[xo, pl.ds(TOK // 2, TOK // 2)], t_recv.at[3])
        fill_near(k)
        dispatch_near(k)
        if k == HOME:
            rows[c, :, HOME * CH:HOME * CH + CAP, :] = near[:, 0:CAP, :]

    def part(xx, k, start=0, size=CH):
        return rows.at[c, xx, pl.ds(k * CH + start, size)]

    def whole(cc, k):
        return rows.at[cc, :, rows_of(k)]

    half = CH // 2

    def gather1(k):
        if k in FAR:
            wait_recv(rows.at[c, x, rows_of(k)], d_recv.at[k])
            mine = part(x, k)
            remote(mine, mine, ga_send.at[0], ga_recv.at[k], e, right).start()
            remote(mine, mine, gb_send.at[0], gb_recv.at[k], e, left).start()
            remote(mine, mine, gs_send.at[0], gs_recv.at[k, 0], e, sib).start()

    def gather2(k):
        if k in FAR:
            low, high = part(xl, k, 0, half), part(xr, k, half, half)
            wait_recv(part(xl, k), ga_recv.at[k])
            remote(low, low, a2_send.at[0], a2_recv.at[k], e, right).start()
            remote(part(xl, k), part(xl, k), gs_send.at[1], gs_recv.at[k, 1], e, sib).start()
            wait_recv(part(xr, k), gb_recv.at[k])
            remote(high, high, b2_send.at[0], b2_recv.at[k], e, left).start()
            remote(part(xr, k), part(xr, k), gs_send.at[2], gs_recv.at[k, 2], e, sib).start()

    def gather3(k):
        if k in FAR:
            wait_recv(part(xo, k, 0, half), a2_recv.at[k])
            wait_recv(part(xo, k, half, half), b2_recv.at[k])
            remote(part(xo, k), part(xo, k), gs_send.at[3], gs_recv.at[k, 3], e, sib).start()
        else:
            wait_recv(rows.at[c, :, others(k)], n_recv.at[k])
            remote(whole(c, k), whole(c, k), gs_send.at[4], gs_recv.at[k, 0], e, sib).start()

    def gather4(k):
        if k in FAR:
            for i in range(4):
                wait_recv(part(x, k), gs_recv.at[k, i])
        else:
            wait_recv(whole(1 - c, k), gs_recv.at[k, 0])

    def eye(first, count):
        return lane[0:count * CH] == sub[0:count * CH] + first % 2 * CH

    def features(hh):
        return pl.ds(pl.multiple_of(hh * FL, FL), FL)

    def group_rows(g):
        first, count = GROUPS[g]
        return pl.ds(first * CH, count * CH)

    def compute(g):
        first, count = GROUPS[g]
        for k in range(first, first + count):
            gather4(k)
        here, high = group_rows(g), count * CH
        pre = jnp.zeros((high, HID), F32)
        back = jnp.zeros((high, HID), F32)
        for hh in range(HEAD):
            part_of = pl.ds(hh * FL, FL)
            pre = pre + nn(rows[hh % 2, hh // 2, here, 0:FL], wup[part_of, :])
            back = back + nn(rows[hh % 2, hh // 2, here, FL:XD], wdn_t[part_of, :])
        for k in range(first, first + count):
            places = sources(k)
            wait_recv(gate_in.at[pl.ds(places[0], len(places))], gl_recv.at[k])
        diagonal = eye(first, count)
        gate = merge(gate_in, first * PER, count * PER)
        g_column = jnp.sum(jnp.where(diagonal, gate, 0.0), axis=1, keepdims=True)
        act, slope = gelu_parts(pre)
        score = jnp.sum(back * act, axis=1, keepdims=True)
        scaled[here, :] = (g_column * act).astype(BF16)
        delta[here, :] = (g_column * back * slope).astype(BF16)
        terms = delta[here, :]
        for xx in range(NX):
            sib_send[xx, here, :] = nn(terms, wup_t[:, features(xx * 2 + (1 - c))]).astype(BF16)
        remote(sib_send.at[:, here], sib_recv.at[:, here], sib_ss.at[g], sib_rs.at[g], e, sib).start()
        line = jnp.sum(jnp.where(diagonal, score, 0.0), axis=0, keepdims=True)
        sc_send[g] = line
        sc_recv[g, h] = line

        def tell(i, carry):
            remote(
                sc_send.at[g], sc_recv.at[g, h], sc_ss.at[g], sc_rs.at[g], e, lax.rem(h + i, HEAD)
            ).start()
            return carry

        lax.fori_loop(1, HEAD, tell, 0)
        for xx in range(NX):
            own[xx, here, :] = nn(terms, wup_t[:, features(xx * 2 + c)])

    def pair(g, xx, start, size):
        here, cols = group_rows(g), pl.ds(start, size)
        return own[xx, here, cols] + sib_recv[xx, here, cols].astype(F32)

    hf = FL // 2

    def reduce1(g):
        here = group_rows(g)
        wait_recv(sib_recv.at[:, here], sib_rs.at[g])
        for i, to in enumerate((right, left)):
            m1s[i, here, :] = pair(g, xo, i * hf, hf).astype(BF16)
            remote(m1s.at[i, here], m1r.at[i, here], m1_ss.at[g, i], m1_rs.at[g, i], e, to).start()

    def reduce2(g):
        here = group_rows(g)
        m2s[0, here, hf:FL] = pair(g, xr, hf, hf).astype(BF16)
        m2s[1, here, 0:hf] = pair(g, xl, 0, hf).astype(BF16)
        for i, (at, to) in enumerate(((xr, right), (xl, left))):
            wait_recv(m1r.at[i, here], m1_rs.at[g, i])
            both = pair(g, at, i * hf, hf) + m1r[i, here, :].astype(F32)
            m2s[i, here, i * hf:(i + 1) * hf] = both.astype(BF16)
            remote(m2s.at[i, here], m2r.at[i, here], m2_ss.at[g, i], m2_rs.at[g, i], e, to).start()

    def reduce3(g):
        here, (first, count) = group_rows(g), GROUPS[g]
        wait_recv(sc_recv.at[g, pl.ds(0, HEAD - 1)], sc_rs.at[g])
        total = sc_recv[g, 0]
        for i in range(1, HEAD):
            total = total + sc_recv[g, i]
        score_lines[g] = total.astype(BF16).astype(F32)
        wait_recv(m2r.at[0, here], m2_rs.at[g, 0])
        wait_recv(m2r.at[1, here], m2_rs.at[g, 1])
        done = pair(g, x, 0, FL) + m2r[0, here, :].astype(F32) + m2r[1, here, :].astype(F32)
        ret_send[here, :] = done.astype(BF16)
        for p in sources(first, count):
            dz, dy = ORDER[p]
            to = exp_of(z + dz, y + dy)
            remote(
                ret_send.at[block(p)], ret_recv.at[block(p)], r_ss.at[0], r_rs.at[g], to, h
            ).start()
            remote(
                score_lines.at[g], score_in.at[p], sl_send.at[0], sl_recv.at[0], to, h
            ).start()
        if first == HOME:
            own_rows = pl.ds(HOME * CH, CAP)
            ret_recv[own_rows, :] = ret_send[own_rows, :]
            score_in[HOME * PER] = score_lines[g]

    def weights_down(k):
        flat = scaled[...].T
        for hh in range(HEAD):
            gdn[0, :, hh * FL:(hh + 1) * FL] = nn(flat, rows[hh % 2, hh // 2, :, FL:XD]).astype(BF16)

    def weights_up(k):
        for hh in range(HEAD):
            gup[0, hh * FL:(hh + 1) * FL, :] = tn(rows[hh % 2, hh // 2, :, 0:FL], delta[...]).astype(BF16)

    stages = {
        "pass": pass_raw, "d": dispatch, "near": send_near, "g1": gather1, "g2": gather2, "g3": gather3,
        "c": compute, "r1": reduce1, "r2": reduce2, "r3": reduce3, "wd": weights_down, "wu": weights_up,
    }
    for stage, k in PLAN:
        stages[stage](k)

    total = jnp.zeros((TOK, FL), F32)
    for g, (first, count) in enumerate(GROUPS):
        here = group_rows(g)
        wait_recv(ret_recv.at[others(first, count)], r_rs.at[g])
        total = total + nn(pt0[:, here] + pt1[:, here], ret_recv[here, :])
    gt_out[...] = total.astype(BF16)
    wait_recv(score_in.at[pl.ds(1, EXP - 1)], sl_recv.at[0])
    for k, pt in enumerate((pt0, pt1)):
        picked = jnp.zeros((TOK, LINE), F32)
        for i in range(ROWS // LINE):
            picked = picked + pt[:, i * LINE:(i + 1) * LINE].astype(F32) * merge(score_in, i * 8, 8)
        score = jnp.sum(picked, axis=1, keepdims=True)
        gg_out[k:k + 1, :] = jnp.sum(jnp.where(lane == sub, score, 0.0), axis=0, keepdims=True).astype(BF16)

    wait_send(raw.at[0], t_send.at[0])
    wait_send(raw.at[0], t_send.at[1])
    wait_send(raw.at[0, pl.ds(0, TOK // 2)], t_send.at[2])
    wait_send(raw.at[0, pl.ds(0, TOK // 2)], t_send.at[3])
    far_rows, near_rows = len(FAR) * CH, len(NEAR) * CH
    wait_send(send.at[pl.ds(0, far_rows)], d_send.at[0])
    wait_send(near.at[:, pl.ds(CAP, near_rows - CAP)], n_send.at[0])
    wait_send(gate_in.at[pl.ds(1, EXP - 1)], gl_send.at[0])
    wait_send(score_in.at[pl.ds(1, EXP - 1)], sl_send.at[0])
    gathered = rows.at[0, 0, pl.ds(0, far_rows)]
    wait_send(gathered, ga_send.at[0])
    wait_send(gathered, gb_send.at[0])
    for i in range(4):
        wait_send(gathered, gs_send.at[i])
    wait_send(rows.at[0, :, pl.ds(0, near_rows)], gs_send.at[4])
    halves = rows.at[0, 0, pl.ds(0, far_rows // 2)]
    wait_send(halves, a2_send.at[0])
    wait_send(halves, b2_send.at[0])
    for g in range(len(GROUPS)):
        here = group_rows(g)
        wait_send(sib_send.at[:, here], sib_ss.at[g])
        for i in range(2):
            wait_send(m1s.at[i, here], m1_ss.at[g, i])
            wait_send(m2s.at[i, here], m2_ss.at[g, i])
        wait_send(sc_recv.at[g, pl.ds(0, HEAD - 1)], sc_ss.at[g])
    wait_send(ret_send.at[pl.ds(CAP, ROWS - CAP)], r_ss.at[0])


CUTS = 4


def store(*refs):
    ins, outs, sem = refs[:4], refs[4:8], refs[8]
    pairs = []
    for i in (2, 3):
        height = ins[i].shape[1] // CUTS
        for j in range(CUTS):
            here = pl.ds(j * height, height)
            pairs.append((ins[i].at[:, here], outs[i].at[:, here]))
    pairs += [(ins[i], outs[i]) for i in (0, 1)]
    copies = [pltpu.make_async_copy(src, dst, sem.at[i]) for i, (src, dst) in enumerate(pairs)]
    for one in copies:
        one.start()
    for one in copies:
        one.wait()


def shards(tokens, cotangent, gates, expert_ids, w_up, w_down):
    vmem = pl.BlockSpec(memory_space=pltpu.VMEM)
    hbm = pl.BlockSpec(memory_space=pl.ANY)
    dma = pltpu.SemaphoreType.DMA
    shapes = ((TOK, FL), (2, TOK), (1, D, HID), (1, HID, D))
    results = pl.pallas_call(
        kernel,
        out_shape=tuple(pltpu.VMEM(shape, BF16) for shape in shapes),
        in_specs=[vmem, vmem, vmem, vmem, hbm, hbm],
        out_specs=(vmem, vmem, vmem, vmem),
        scratch_shapes=[
            pltpu.VMEM((D, HID), BF16),
            pltpu.VMEM((HID, D), BF16),
            pltpu.VMEM((HID, D), BF16),
            pltpu.VMEM((D, HID), BF16),
            pltpu.VMEM((TOK, ROWS), BF16),
            pltpu.VMEM((TOK, ROWS), BF16),
            pltpu.VMEM((NX, TOK, XD), BF16),
            pltpu.VMEM((ROWS, XD), BF16),
            pltpu.VMEM((NX, len(NEAR) * CH, XD), BF16),
            pltpu.VMEM((2, NX, ROWS, XD), BF16),
            pltpu.VMEM((ROWS // LINE, 1, LINE), F32),
            pltpu.VMEM((EXP, 1, LINE), F32),
            pltpu.VMEM((NCH, 1, LINE), F32),
            pltpu.VMEM((EXP, 1, LINE), F32),
            pltpu.VMEM((ROWS, HID), BF16),
            pltpu.VMEM((ROWS, HID), BF16),
            pltpu.VMEM((NX, ROWS, FL), BF16),
            pltpu.VMEM((NX, ROWS, FL), BF16),
            pltpu.VMEM((NX, ROWS, FL), F32),
            pltpu.VMEM((2, ROWS, FL // 2), BF16),
            pltpu.VMEM((2, ROWS, FL // 2), BF16),
            pltpu.VMEM((2, ROWS, FL), BF16),
            pltpu.VMEM((2, ROWS, FL), BF16),
            pltpu.VMEM((NCH, 1, LINE), F32),
            pltpu.VMEM((NCH, HEAD, 1, LINE), F32),
            pltpu.VMEM((ROWS, FL), BF16),
            pltpu.VMEM((ROWS, FL), BF16),
            dma((2,)),
            dma((4,)), dma((4,)),
            dma((1,)), dma((NCH,)),
            dma((1,)), dma((NCH,)),
            dma((1,)), dma((NCH,)),
            dma((1,)), dma((1,)),
            dma((1,)), dma((NCH,)),
            dma((1,)), dma((NCH,)),
            dma((1,)), dma((NCH,)),
            dma((1,)), dma((NCH,)),
            dma((5,)), dma((NCH, 4)),
            dma((NCH,)), dma((NCH,)),
            dma((NCH, 2)), dma((NCH, 2)),
            dma((NCH, 2)), dma((NCH, 2)),
            dma((NCH,)), dma((NCH,)),
            dma((1,)), dma((NCH,)),
        ],
        compiler_params=pltpu.CompilerParams(
            collective_id=0, has_side_effects=True, vmem_limit_bytes=56 * 1024 * 1024
        ),
        cost_estimate=pl.CostEstimate(
            flops=10 * ROWS * D * HID, bytes_accessed=8 * D * HID, transcendentals=2 * ROWS * HID
        ),
    )(tokens, cotangent, gates.T, expert_ids.T, w_up, w_down)
    grad_tokens, grad_gates, grad_up, grad_down = pl.pallas_call(
        store,
        out_shape=tuple(jax.ShapeDtypeStruct(shape, BF16) for shape in shapes),
        in_specs=[vmem] * 4,
        out_specs=(hbm,) * 4,
        scratch_shapes=[dma((2 * CUTS + 2,))],
        compiler_params=pltpu.CompilerParams(vmem_limit_bytes=16 * 1024 * 1024),
    )(*results)
    return grad_tokens, grad_gates.T, grad_up, grad_down


def solution(mesh):
    return jax.shard_map(
        shards,
        mesh=mesh,
        in_specs=(
            P("exp", "head"),
            P("exp", "head"),
            P("exp", None),
            P("exp", None),
            P("exp", None, "head"),
            P("exp", "head", None),
        ),
        out_specs=(
            P("exp", "head"),
            P("exp", None),
            P("exp", None, "head"),
            P("exp", "head", None),
        ),
        check_vma=False,
    )
```
